256 devices in a mesh: panel: 2 (over x_lo), lat: 16 (over z, core), lon: 8 (over y, x_hi).
Axes of the slice: x: 4 (x_hi: 2, x_lo: 2; x = x_hi * 2 + x_lo), y: 4, z: 8, core: 2. Of those that a mesh axis runs over, the one named last changes fastest.
Arguments:
- state: float32 [2, 7, 2, 384, 4608], P('panel', None, None, 'lat', 'lon'), may hold values from -4 to 4
- pack_cell: int32 [2, 16, 8, 48], P('panel', 'lat', 'lon'), may hold values from 0 to 13224, as said below
- pack_frac: float32 [2, 2, 16, 8, 48], P('panel', None, 'lat', 'lon'), may hold values from 0 to 1
- ns_source: int32 [2, 2, 4608], P(None, None, 'lon'), may hold values from 0 to 6143
- we_source: int32 [2, 2, 384], P(None, None, 'lat'), may hold values from 0 to 6143
- ns_turn: float32 [2, 2, 4608], P(None, None, 'lon'), may hold values from -3.140625 to 3.140625
- we_turn: float32 [2, 2, 384], P(None, None, 'lat'), may hold values from -3.140625 to 3.140625
Outputs:
- new_state: float32 [2, 7, 2, 384, 4608], P('panel', None, None, 'lat', 'lon')
The draws below stay inside these ranges and needn't reach their ends.
Inputs may be any that keep to these rules, and one draw needn't show every extreme that they name: `pack_cell`: donor offsets leave room for the next row and column inside the tile.
All inputs are finite; a program needn't handle non-finite values.
Results may differ from the reference program's by a relative error of at most 0.00002.
Values sent between devices are 32-bit elements; how exact they have to be, the bound alone decides.
No kernel may reach another device: no remote copies, remote signals or barrier semaphores. Data moves between devices by JAX's collectives and lax.ppermute only.
A program may use at most 128 MiB of HBM per device.

```python
import math
import jax
import jax.numpy as jnp

R = 2
CT = 24
CP = 576
SLOTS = 48
NT = 384
NP = 4608
TILES = 128
N_LAT = 16
N_LON = 8


def draw_state(key, part):
    key = jax.random.fold_in(key, 5)
    key_inner, key_rim, key_sign = jax.random.split(key, 3)
    shape = (2, 7, R, NT, NP)
    inner = jnp.clip(0.7 * jax.random.normal(key_inner, shape, jnp.float32), -4.0, 4.0)
    magnitude = jax.random.uniform(key_rim, shape, jnp.float32, 2.5, 4.0)
    flips = jax.random.randint(key_sign, shape, 0, 2)
    signed = jnp.where(flips == 1, magnitude, -magnitude)
    row_index = jnp.arange(NT, dtype=jnp.int32)[:, None]
    col_index = jnp.arange(NP, dtype=jnp.int32)[None, :]
    outer = (row_index == 0) | (row_index == NT - 1) | (col_index == 0) | (col_index == NP - 1)
    return jnp.where(outer, signed, inner).astype(jnp.float32)


def draw_pack_cell(key, part):
    key = jax.random.fold_in(key, 11)
    key_base, key_along, key_down = jax.random.split(key, 3)
    shape = (2, N_LAT, N_LON, SLOTS)
    base = jax.random.randint(key_base, shape, 0, (CT - 1) * (CP - 1))
    along_row = jax.random.randint(key_along, shape, 0, CP - 1)
    along_col = jax.random.randint(key_down, shape, 0, CT - 1)
    tile_a = jnp.arange(N_LAT, dtype=jnp.int32)[None, :, None, None]
    tile_b = jnp.arange(N_LON, dtype=jnp.int32)[None, None, :, None]
    slot_index = jnp.arange(SLOTS, dtype=jnp.int32)[None, None, None, :]
    north_cell = along_row
    south_cell = (CT - 2) * (CP - 1) + along_row
    west_cell = along_col * (CP - 1)
    east_cell = along_col * (CP - 1) + CP - 2
    edge_cell = jnp.where(tile_a == 0, north_cell, jnp.where(tile_a == N_LAT - 1, south_cell, jnp.where(tile_b == 0, west_cell, east_cell)))
    on_edge = (tile_a == 0) | (tile_a == N_LAT - 1) | (tile_b == 0) | (tile_b == N_LON - 1)
    half_slots = max(SLOTS // 2, 1)
    chosen = on_edge & (slot_index < half_slots)
    cells = jnp.where(chosen, edge_cell, base)
    cells = cells.at[0, 0, 0, 0].set(0)
    cells = cells.at[1, N_LAT - 1, N_LON - 1, SLOTS - 1].set((CT - 1) * (CP - 1) - 1)
    return cells.astype(jnp.int32)


def source_list(key, length):
    keys = jax.random.split(key, 6)
    shape = (2, 2, length)
    coin = jax.random.randint(keys[0], shape, 0, 2)
    side = jax.random.randint(keys[1], shape, 0, 4)
    row_pick = jax.random.randint(keys[2], shape, 0, N_LAT)
    col_pick = jax.random.randint(keys[3], shape, 0, N_LON)
    half_slots = max(SLOTS // 2, 1)
    edge_slot = jax.random.randint(keys[4], shape, 0, half_slots)
    any_slot = jax.random.randint(keys[5], shape, 0, SLOTS)
    edge_a = jnp.where(side == 0, 0, jnp.where(side == 1, N_LAT - 1, row_pick))
    edge_b = jnp.where(side == 2, 0, jnp.where(side == 3, N_LON - 1, col_pick))
    tile_a = jnp.where(coin == 1, edge_a, row_pick)
    tile_b = jnp.where(coin == 1, edge_b, col_pick)
    slot_pick = jnp.where(coin == 1, edge_slot, any_slot)
    sources = (tile_a * N_LON + tile_b) * SLOTS + slot_pick
    sources = sources.at[0, 0, 0].set(0)
    sources = sources.at[1, 1, length - 1].set(TILES * SLOTS - 1)
    return sources.astype(jnp.int32)


def draw_ns_source(key, part):
    key = jax.random.fold_in(key, 23)
    return source_list(key, NP)


def draw_we_source(key, part):
    key = jax.random.fold_in(key, 37)
    return source_list(key, NT)


def shard_levels(key, shape, shards, least, high):
    loudness = 1.0
    for dim, blocks in shards:
        heights = jax.random.uniform(jax.random.fold_in(jax.random.fold_in(key, 6), dim), (blocks,), jnp.float32, least / len(shards), high / len(shards))
        loudness = loudness * jnp.repeat(jnp.exp(heights), shape[dim] // blocks).reshape((-1,) + (1,) * (len(shape) - 1 - dim))
    return loudness


def setup_inputs(seed: int = 0) -> dict:
    arg_keys = jax.random.split(jax.random.key(seed), 8)
    state = draw_state(jax.random.fold_in(arg_keys[7], 71), 0)
    pack_cell = draw_pack_cell(jax.random.fold_in(arg_keys[7], 71), 0)
    pack_frac = jnp.clip(1.0 * jax.random.uniform(arg_keys[2], (2, 2, N_LAT, N_LON, SLOTS), jnp.float32) ** shard_levels(arg_keys[2], (2, 2, N_LAT, N_LON, SLOTS), ((0, 2), (2, 16), (3, 8)), -0.2, 0.2), 0.0, 1.0)
    ns_source = draw_ns_source(jax.random.fold_in(arg_keys[7], 71), 0)
    we_source = draw_we_source(jax.random.fold_in(arg_keys[7], 71), 0)
    ns_turn = jnp.clip(jax.random.uniform(arg_keys[5], (2, 2, NP), jnp.float32, -3.140625, 3.140625), -3.140625, 3.140625)
    we_turn = jnp.clip(jax.random.uniform(arg_keys[6], (2, 2, NT), jnp.float32, -3.140625, 3.140625), -3.140625, 3.140625)
    return {"state": state, "pack_cell": pack_cell, "pack_frac": pack_frac, "ns_source": ns_source, "we_source": we_source, "ns_turn": ns_turn, "we_turn": we_turn}


time_step = 0.25
viscosity = 0.1
resistivity = 0.08
conduction = 0.12
buoyancy = 0.5
gradient = 0.5


def tendency(ghosted, inv_sine):
    padded = jnp.pad(ghosted, ((0, 0), (1, 1), (0, 0), (0, 0)))
    centre = padded[:, 1:-1, 1:-1, 1:-1]
    above_r = padded[:, 2:, 1:-1, 1:-1]
    below_r = padded[:, :-2, 1:-1, 1:-1]
    north_side = padded[:, 1:-1, :-2, 1:-1]
    south_side = padded[:, 1:-1, 2:, 1:-1]
    west_side = padded[:, 1:-1, 1:-1, :-2]
    east_side = padded[:, 1:-1, 1:-1, 2:]
    metric = inv_sine[None, None, :, None]
    grad_r = 0.5 * (above_r - below_r)
    grad_t = 0.5 * (south_side - north_side)
    grad_p = 0.5 * metric * (east_side - west_side)
    laplace = (above_r + below_r - 2.0 * centre) + (south_side + north_side - 2.0 * centre) + metric * metric * (east_side + west_side - 2.0 * centre)
    by_flow = centre[0:1] * grad_r + centre[1:2] * grad_t + centre[2:3] * grad_p
    by_field = centre[3:4] * grad_r + centre[4:5] * grad_t + centre[5:6] * grad_p
    velocity = -by_flow[0:3] + by_field[3:6] + viscosity * laplace[0:3]
    velocity = velocity.at[0].add(buoyancy * centre[6])
    magnetic = -by_flow[3:6] + by_field[0:3] + resistivity * laplace[3:6]
    thermal = -by_flow[6:7] + conduction * laplace[6:7] + gradient * centre[0:1]
    return jnp.concatenate([velocity, magnetic, thermal], 0)


def rotate(values, angle):
    cosine = jnp.cos(angle)
    sine = jnp.sin(angle)
    return jnp.stack([values[0], cosine * values[1] - sine * values[2], sine * values[1] + cosine * values[2],
                      values[3], cosine * values[4] - sine * values[5], sine * values[4] + cosine * values[5], values[6]])


def pick_rim(donated, source, angle, layers):
    taken = jnp.take(donated, source.reshape(-1), axis=1)
    taken = taken.reshape(7, layers, source.shape[0], source.shape[1])
    return rotate(taken, angle)


def panel_packets(panel, donor_cell, fractions):
    flat = panel.reshape(7 * R, NT * NP)
    lat_off = donor_cell // (CP - 1)
    lon_off = donor_cell % (CP - 1)
    tile_row = jnp.arange(N_LAT, dtype=jnp.int32)[:, None, None] * CT
    tile_col = jnp.arange(N_LON, dtype=jnp.int32)[None, :, None] * CP
    start = ((tile_row + lat_off) * NP + tile_col + lon_off).reshape(-1).astype(jnp.int32)
    frac_a = fractions[0].reshape(-1)
    frac_b = fractions[1].reshape(-1)
    return ((1.0 - frac_a) * (1.0 - frac_b) * jnp.take(flat, start, axis=1)
            + (1.0 - frac_a) * frac_b * jnp.take(flat, start + 1, axis=1)
            + frac_a * (1.0 - frac_b) * jnp.take(flat, start + NP, axis=1)
            + frac_a * frac_b * jnp.take(flat, start + NP + 1, axis=1))


def full_tendency(section, pack_cell, pack_frac, ns_source, we_source, ns_turn, we_turn, inv_sine):
    packets = [panel_packets(section[0], pack_cell[0], pack_frac[0]), panel_packets(section[1], pack_cell[1], pack_frac[1])]
    results = []
    for panel_index in range(2):
        donated = packets[1 - panel_index]
        cycle_ns = pick_rim(donated, ns_source[panel_index], ns_turn[panel_index], R)
        cycle_we = pick_rim(donated, we_source[panel_index], we_turn[panel_index], R)
        ghosted = jnp.pad(section[panel_index], ((0, 0), (0, 0), (1, 1), (1, 1)))
        ghosted = ghosted.at[:, :, 0, 1:-1].set(cycle_ns[:, :, 0])
        ghosted = ghosted.at[:, :, -1, 1:-1].set(cycle_ns[:, :, 1])
        ghosted = ghosted.at[:, :, 1:-1, 0].set(cycle_we[:, :, 0])
        ghosted = ghosted.at[:, :, 1:-1, -1].set(cycle_we[:, :, 1])
        results.append(tendency(ghosted, inv_sine))
    return jnp.stack(results)


def reference(state, pack_cell, pack_frac, ns_source, we_source, ns_turn, we_turn):
    rows = jnp.arange(NT, dtype=jnp.int32).astype(jnp.float32)
    theta = math.pi / 4 + (rows + 0.5) * (math.pi / 2) / NT
    inv_sine = 1.0 / jnp.sin(theta)

    def evaluate(section):
        return full_tendency(section, pack_cell, pack_frac, ns_source, we_source, ns_turn, we_turn, inv_sine)

    first = evaluate(state)
    second = evaluate(state + (time_step / 2) * first)
    third = evaluate(state + (time_step / 2) * second)
    fourth = evaluate(state + time_step * third)
    return state + (time_step / 6) * (first + 2.0 * second + 2.0 * third + fourth)
```

```python
import functools
import math

import jax
import jax.numpy as jnp
from jax import lax
from jax.experimental import pallas as pl
from jax.experimental.pallas import tpu as pltpu
from jax.sharding import Mesh, PartitionSpec as P

time_step = 0.25
viscosity = 0.1
resistivity = 0.08
conduction = 0.12
buoyancy = 0.5
gradient = 0.5

AXES = ("panel", "z", "core", "y", "xh")
SIZES = dict(zip(AXES, (2, 8, 2, 4, 2)))
LAT = ("z", "core")
LON = ("y", "xh")

FIELDS = 14
CT = 24
CP = 576
ROWS = 32
COLS = 640
HALO = 4
SLOTS = 48
NT = 384
LANES = 128
TILES = 128
LANE_TILES = COLS // LANES
LAST = COLS - LANES
VMEM_LIMIT = 24 * 1024 * 1024


def lane_of(shape):
    return lax.broadcasted_iota(jnp.int32, shape, len(shape) - 1)


def row_of(shape):
    return lax.broadcasted_iota(jnp.int32, shape, len(shape) - 2)


def lane_gather(block, index):
    return jnp.take_along_axis(block, index, axis=1, mode="promise_in_bounds")


def build_packet(block_of, index_ref, weight_ref):
    left = lane_of((1, LANES)) < 64
    sums = []
    for f in range(FIELDS):
        total = None
        for t in range(LANE_TILES):
            index = index_ref[t]
            for rb in range(CT // 8):
                term = weight_ref[rb * LANE_TILES + t] * lane_gather(block_of(f, rb, t), index)
                total = term if total is None else total + term
        row = jnp.sum(total, axis=0, keepdims=True)
        sums.append(row + pltpu.roll(row, 64, 1))
    zero = jnp.zeros((1, LANES), jnp.float32)
    rows = [jnp.where(left, sums[f], sums[f + 8] if f + 8 < FIELDS else zero) for f in range(8)]
    return jnp.concatenate(rows, axis=0)


def state_block(state_ref, f, rb, t):
    rows = slice(rb * 8, rb * 8 + 8)
    if t < LANE_TILES - 1:
        return state_ref[f, rows, t * LANES : (t + 1) * LANES]
    half = state_ref[f, rows, LAST:CP]
    return jnp.concatenate([half, jnp.zeros((8, LANES - 64), jnp.float32)], axis=1)


def open_kernel(state_ref, aux_ref, packet_ref, north_ref, south_ref, index_ref, weight_ref):
    shape = (8, LANES)
    lane = lane_of(shape)
    row = row_of(shape)
    cell = jnp.broadcast_to(aux_ref[4:5, 0:LANES], shape)
    frac_u = jnp.broadcast_to(aux_ref[5:6, 0:LANES], shape)
    frac_v = jnp.broadcast_to(aux_ref[6:7, 0:LANES], shape)
    lat_off = jnp.floor((cell + 0.5) * (1.0 / (CP - 1)))
    lon_off = cell - lat_off * (CP - 1)
    lat_off = lat_off.astype(jnp.int32)
    second = lane >= 64
    column = lon_off.astype(jnp.int32) + second.astype(jnp.int32)
    used = (lane & 63) < SLOTS
    along = jnp.where(second, frac_v, 1.0 - frac_v)
    for t in range(LANE_TILES):
        local = column - t * LANES
        inside = used & (local >= 0) & (local < LANES)
        index_ref[t] = jnp.where(inside, local, 0)
        for rb in range(CT // 8):
            here = row + rb * 8
            down = jnp.where(here == lat_off, 1.0 - frac_u, jnp.where(here == lat_off + 1, frac_u, 0.0))
            weight_ref[rb * LANE_TILES + t] = jnp.where(inside, down * along, 0.0)
    packet_ref[...] = build_packet(functools.partial(state_block, state_ref), index_ref, weight_ref)
    upper = row_of((8, COLS)) < HALO
    for c in range(7):
        for t in range(LANE_TILES):
            cols = slice(t * LANES, (t + 1) * LANES)
            top = [state_block(state_ref, 2 * c + k, 0, t) for k in range(2)]
            end = [state_block(state_ref, 2 * c + k, CT // 8 - 1, t) for k in range(2)]
            north_ref[c, :, cols] = jnp.where(row < HALO, top[0], pltpu.roll(top[1], HALO, 0))
            south_ref[c, :, cols] = jnp.where(row < HALO, pltpu.roll(end[0], HALO, 0), end[1])
    north_ref[7] = aux_ref[...]
    south_ref[7] = aux_ref[...]


def outer_rows(from_south, from_north, k, row):
    if k == 0:
        return jnp.where(row < HALO, from_south, pltpu.roll(from_north, HALO, 0))
    return jnp.where(row < HALO, pltpu.roll(from_south, HALO, 0), from_north)


def side_kernel(state_ref, from_south_ref, from_north_ref, aux_ref, west_ref, east_ref):
    shape = (8, LANES)
    lane = lane_of(shape)
    row = row_of(shape)
    for rb in range(ROWS // 8):
        west = jnp.zeros(shape, jnp.float32)
        east = jnp.zeros(shape, jnp.float32)
        for f in range(FIELDS):
            c, k = f // 2, f % 2
            if rb < CT // 8:
                first = state_block(state_ref, f, rb, 0)
                last = state_block(state_ref, f, rb, LANE_TILES - 1)
            else:
                first = outer_rows(from_south_ref[c, :, 0:LANES], from_north_ref[c, :, 0:LANES], k, row)
                last = outer_rows(from_south_ref[c, :, LAST:COLS], from_north_ref[c, :, LAST:COLS], k, row)
            here = (lane >= 8 * f) & (lane < 8 * f + HALO)
            west = jnp.where(here, pltpu.roll(first, 8 * f, 1) if f else first, west)
            east = jnp.where(here, pltpu.roll(last, (8 * f - 60) % LANES, 1), east)
        if rb == 0:
            here = (lane >= 112) & (lane < 112 + HALO)
            west = jnp.where(here, pltpu.roll(aux_ref[:, 0:LANES], 112, 1), west)
            east = jnp.where(here, pltpu.roll(aux_ref[:, LAST:COLS], 112 - 60, 1), east)
        west_ref[rb * 8 : rb * 8 + 8, :] = west
        east_ref[rb * 8 : rb * 8 + 8, :] = east


def frame_kernel(
    flags_ref, state_ref, from_south_ref, from_north_ref, from_east_ref, from_west_ref, aux_ref,
    full_ref, slot_ref, tile_ref, cos_ref, sin_ref, metric_ref,
):
    shape = (8, LANES)
    lane = lane_of(shape)
    row = row_of(shape)
    for rb in range(ROWS // 8):
        rows = slice(rb * 8, rb * 8 + 8)
        from_east = from_east_ref[rows, :]
        from_west = from_west_ref[rows, :]
        for f in range(FIELDS):
            c, k = f // 2, f % 2
            for t in range(LANE_TILES):
                cols = slice(t * LANES, (t + 1) * LANES)
                if rb < CT // 8:
                    block = state_block(state_ref, f, rb, t)
                else:
                    block = outer_rows(from_south_ref[c, :, cols], from_north_ref[c, :, cols], k, row)
                if t == LANE_TILES - 1:
                    block = jnp.where((lane >= 64) & (lane < 64 + HALO), pltpu.roll(from_east, (64 - 8 * f) % LANES, 1), block)
                    block = jnp.where(lane >= LANES - HALO, pltpu.roll(from_west, (124 - 8 * f) % LANES, 1), block)
                full_ref[f, rows, cols] = block
    mine = flags_ref[2]
    for t in range(LANE_TILES + 1):
        if t < LANE_TILES:
            block = aux_ref[:, t * LANES : (t + 1) * LANES]
            if t == LANE_TILES - 1:
                east = from_east_ref[0:8, :]
                west = from_west_ref[0:8, :]
                block = jnp.where((lane >= 64) & (lane < 64 + HALO), pltpu.roll(east, (64 - 112) % LANES, 1), block)
                block = jnp.where(lane >= LANES - HALO, pltpu.roll(west, 124 - 112, 1), block)
            source = jnp.broadcast_to(block[0:1, :], shape)
            angle = jnp.broadcast_to(block[1:2, :], shape)
        else:
            block = aux_ref[:, 0:LANES]
            block = jnp.where((lane >= CT) & (lane < CT + HALO), pltpu.roll(from_south_ref[7, :, 0:LANES], CT, 1), block)
            block = jnp.where((lane >= 28) & (lane < 32), pltpu.roll(from_north_ref[7, :, 0:LANES], 8, 1), block)
            source = jnp.broadcast_to(block[2:3, :], shape)
            angle = jnp.broadcast_to(block[3:4, :], shape)
        whole = jnp.floor((source + 0.5) * (1.0 / SLOTS))
        slot_ref[t] = (source - whole * SLOTS).astype(jnp.int32)
        tile_ref[t] = whole.astype(jnp.int32) ^ mine
        cos_ref[t] = jnp.cos(angle)
        sin_ref[t] = jnp.sin(angle)
    line = row_of((ROWS, LANES))
    line = jnp.where(line >= ROWS - HALO, line - ROWS, line) + flags_ref[0] * CT
    theta = math.pi / 4 + (line.astype(jnp.float32) + 0.5) * ((math.pi / 2) / NT)
    metric_ref[...] = 1.0 / jnp.sin(theta)


def pick_ghosts(donor_ref, slot_ref, tile_ref, cos_ref, sin_ref):
    shape = (8, LANES)
    row = row_of(shape)
    count = LANE_TILES + 1
    slots = [slot_ref[t] for t in range(count)]
    tiles = [tile_ref[t] for t in range(count)]
    low = [jnp.zeros(shape, jnp.float32) for _ in range(count)]
    high = [jnp.zeros(shape, jnp.float32) for _ in range(count)]
    for v in range(TILES):
        z, core, y, x = v // 16, v // 8 % 2, v // 2 % 4, v % 2
        block = donor_ref[core, z * 4 + y, x]
        for t in range(count):
            here = tiles[t] == v
            low[t] = jnp.where(here, lane_gather(block, slots[t]), low[t])
            high[t] = jnp.where(here, lane_gather(block, slots[t] + 64), high[t])
    ghosts = []
    for t in range(count):
        cosine, sine = cos_ref[t], sin_ref[t]
        first = (row == 2) | (row == 3)
        other = (row == 4) | (row == 5)
        mate = jnp.where(first, pltpu.roll(low[t], 6, 0), pltpu.roll(low[t], 2, 0))
        turn = jnp.where(first, -sine, sine)
        a = jnp.where(first | other, cosine * low[t] + turn * mate, low[t])
        first = row < 2
        mate = jnp.where(first, pltpu.roll(high[t], 6, 0), pltpu.roll(high[t], 2, 0))
        turn = jnp.where(first, -sine, sine)
        b = jnp.where(row < 4, cosine * high[t] + turn * mate, high[t])
        ghosts.append((a, b))
    return ghosts


def put_ghosts(flags_ref, work_ref, ghosts):
    lat, lon = flags_ref[0], flags_ref[1]

    def put_row(line):
        for f in range(FIELDS):
            for t in range(LANE_TILES):
                work_ref[f, line : line + 1, t * LANES : (t + 1) * LANES] = ghosts[t][f // 8][f % 8 : f % 8 + 1, :]

    def put_column(place):
        shape = (ROWS, LANES)
        lane = lane_of(shape)
        diagonal = lane == row_of(shape)
        for f in range(FIELDS):
            values = jnp.broadcast_to(ghosts[LANE_TILES][f // 8][f % 8 : f % 8 + 1, :], shape)
            column = jnp.sum(jnp.where(diagonal, values, 0.0), axis=1, keepdims=True)
            work_ref[f, :, LAST:COLS] = jnp.where(lane == place, jnp.broadcast_to(column, shape), work_ref[f, :, LAST:COLS])

    pl.when(lat == 0)(lambda: put_row(ROWS - 1))
    pl.when(lat == NT // CT - 1)(lambda: put_row(CT))
    pl.when(lon == 0)(lambda: put_column(LANES - 1))
    pl.when(lon == 7)(lambda: put_column(CP - LAST))


def tendency(work_ref, metric_ref, rb, k, emit):
    low = rb * 8
    rows = slice(low, low + 8)
    shape = (8, COLS)
    row = row_of(shape)
    metric = jnp.concatenate([metric_ref[rows, :]] * LANE_TILES, axis=1)
    square = metric * metric
    centre_weight = 4.0 + 2.0 * square
    radial = 0.5 if k == 0 else -0.5

    def value(c):
        return work_ref[2 * c + k, rows, :]

    def coefficients(c):
        return radial * value(c), 0.5 * value(c + 1), (0.5 * metric) * value(c + 2)

    flow_by = coefficients(0)
    field_by = coefficients(3)

    def parts(c):
        f = 2 * c + k
        centre = value(c)
        across = work_ref[2 * c + 1 - k, rows, :]
        before = (low - 1) % ROWS
        after = (low + 8) % ROWS
        north = jnp.where(row == 0, jnp.broadcast_to(work_ref[f, before : before + 1, :], shape), pltpu.roll(centre, 1, 0))
        south = jnp.where(row == 7, jnp.broadcast_to(work_ref[f, after : after + 1, :], shape), pltpu.roll(centre, 7, 0))
        west = pltpu.roll(centre, 1, 1)
        east = pltpu.roll(centre, COLS - 1, 1)
        grad_t = south - north
        grad_p = east - west
        laplace = across + (south + north) + square * (east + west) - centre_weight * centre
        return across, grad_t, grad_p, laplace

    def along(by, p):
        return by[0] * p[0] + by[1] * p[1] + by[2] * p[2]

    for c in range(3):
        p = parts(c)
        u_flow, u_field, u_laplace = along(flow_by, p), along(field_by, p), p[3]
        p = parts(c + 3)
        velocity = along(field_by, p) - u_flow + viscosity * u_laplace
        if c == 0:
            velocity = velocity + buoyancy * value(6)
        emit(c, velocity)
        emit(c + 3, u_field - along(flow_by, p) + resistivity * p[3])
    p = parts(6)
    emit(6, conduction * p[3] - along(flow_by, p) + gradient * value(0))


def stage_kernel(
    factor, flags_ref, donor_ref, slot_ref, tile_ref, cos_ref, sin_ref, metric_ref, index_ref, weight_ref, full_ref, now_ref,
    next_ref, packet_ref, work_ref,
):
    work_ref[...] = now_ref[...]
    put_ghosts(flags_ref, work_ref, pick_ghosts(donor_ref, slot_ref, tile_ref, cos_ref, sin_ref))
    for rb in range(ROWS // 8):
        rows = slice(rb * 8, rb * 8 + 8)
        for k in range(2):

            def emit(c, value):
                next_ref[2 * c + k, rows, :] = full_ref[2 * c + k, rows, :] + factor * value

            tendency(work_ref, metric_ref, rb, k, emit)

    def block_of(f, rb, t):
        return next_ref[f, rb * 8 : rb * 8 + 8, t * LANES : (t + 1) * LANES]

    packet_ref[...] = build_packet(block_of, index_ref, weight_ref)


def last_kernel(
    flags_ref, donor_ref, slot_ref, tile_ref, cos_ref, sin_ref, metric_ref, full_ref, second_ref, third_ref, fourth_ref,
    out_ref, work_ref,
):
    work_ref[...] = fourth_ref[...]
    put_ghosts(flags_ref, work_ref, pick_ghosts(donor_ref, slot_ref, tile_ref, cos_ref, sin_ref))
    for rb in range(CT // 8):
        rows = slice(rb * 8, rb * 8 + 8)
        for k in range(2):

            def emit(c, value):
                f = 2 * c + k
                base = second_ref[f, rows, :] + 2.0 * third_ref[f, rows, :] + fourth_ref[f, rows, :] - full_ref[f, rows, :]
                out_ref[f, rows, :] = ((1.0 / 3.0) * base + (time_step / 6) * value)[:, :CP]

            tendency(work_ref, metric_ref, rb, k, emit)


def call(kernel, ins, outs, scratch=(), flags=False):
    vmem = pl.BlockSpec(memory_space=pltpu.VMEM)
    specs = [vmem] * len(ins)
    if flags:
        specs[0] = pl.BlockSpec(memory_space=pltpu.SMEM)
    shapes = tuple(jax.ShapeDtypeStruct(s, d) for s, d in outs)
    return pl.pallas_call(
        kernel,
        out_shape=shapes,
        in_specs=specs,
        out_specs=(vmem,) * len(outs),
        scratch_shapes=list(scratch),
        compiler_params=pltpu.CompilerParams(vmem_limit_bytes=VMEM_LIMIT),
    )(*ins)


def coordinates(axes):
    points = [()]
    for a in axes:
        points = [q + (i,) for q in points for i in range(SIZES[a])]
    return points


def permute(value, axes, move):
    points = coordinates(axes)
    place = {q: i for i, q in enumerate(points)}
    pairs = []
    for q in points:
        to = move(q)
        if to is not None:
            pairs.append((place[q], place[to]))
    return lax.ppermute(value, axes if len(axes) > 1 else axes[0], pairs)


def shifted(value, axes, step):
    inner = SIZES[axes[1]]
    count = SIZES[axes[0]] * inner

    def move(q):
        to = q[0] * inner + q[1] + step
        return (to // inner, to % inner) if 0 <= to < count else None

    return permute(value, axes, move)


def gather_packets(packet):
    same = permute(packet, ("panel", "xh"), lambda q: (1 - q[0], q[1]))
    other = permute(packet, ("panel", "xh"), lambda q: (1 - q[0], 1 - q[1]))
    both = jnp.stack([same, other])
    count = SIZES["z"] * SIZES["y"]
    spread = lax.all_to_all(jnp.broadcast_to(both[None], (count,) + both.shape), ("z", "y"), 0, 0)
    return lax.all_gather(spread, "core")


def on_device(state, pack_cell, pack_frac, ns_source, we_source, ns_turn, we_turn):
    f32 = jnp.float32
    tile = state.reshape(FIELDS, CT, CP)
    lat = lax.axis_index(LAT)
    lon = lax.axis_index(LON)
    panel = lax.axis_index("panel")
    flags = jnp.stack([lat, lon, lax.axis_index("xh")]).astype(jnp.int32)
    side_ns = (lat == SIZES["z"] * SIZES["core"] - 1).astype(jnp.int32)
    side_we = (lon == SIZES["y"] * SIZES["xh"] - 1).astype(jnp.int32)

    def chosen(table, side):
        line = lax.dynamic_slice(table, (panel, side, 0), (1, 1, table.shape[2]))[0].astype(f32)
        return jnp.pad(line, ((0, 0), (0, COLS - line.shape[1])))

    def doubled(line):
        line = line.reshape(1, SLOTS).astype(f32)
        return jnp.pad(line, ((0, 0), (0, COLS - SLOTS))) + jnp.pad(line, ((0, 0), (64, COLS - 64 - SLOTS)))

    fractions = pack_frac.reshape(2, SLOTS)
    aux = jnp.concatenate(
        [
            chosen(ns_source, side_ns),
            chosen(ns_turn, side_ns),
            chosen(we_source, side_we),
            chosen(we_turn, side_we),
            doubled(pack_cell),
            doubled(fractions[0]),
            doubled(fractions[1]),
            jnp.zeros((1, COLS), f32),
        ],
        axis=0,
    )
    vreg = (8, LANES)
    full_shape = (FIELDS, ROWS, COLS)
    message = (8, 8, COLS)
    packet, to_north, to_south, index, weight = call(
        open_kernel,
        [tile, aux],
        [(vreg, f32), (message, f32), (message, f32), ((LANE_TILES,) + vreg, jnp.int32), ((3 * LANE_TILES,) + vreg, f32)],
    )
    from_south = shifted(to_north, LAT, -1)
    from_north = shifted(to_south, LAT, 1)
    donors = gather_packets(packet)
    to_west, to_east = call(side_kernel, [tile, from_south, from_north, aux], [((ROWS, LANES), f32)] * 2)
    from_east = shifted(to_west, LON, -1)
    from_west = shifted(to_east, LON, 1)
    points = (LANE_TILES + 1,) + vreg
    full, slot, where, cosine, sine, metric = call(
        frame_kernel,
        [flags, tile, from_south, from_north, from_east, from_west, aux],
        [(full_shape, f32), (points, jnp.int32), (points, jnp.int32), (points, f32), (points, f32), ((ROWS, LANES), f32)],
        flags=True,
    )
    ghost_tables = [slot, where, cosine, sine, metric]
    work = [pltpu.VMEM(full_shape, f32)]
    states = [full]
    for factor in (time_step / 2, time_step / 2, time_step):
        after, packet = call(
            functools.partial(stage_kernel, factor),
            [flags, donors] + ghost_tables + [index, weight, full, states[-1]],
            [(full_shape, f32), (vreg, f32)],
            work,
            flags=True,
        )
        states.append(after)
        donors = gather_packets(packet)
    (result,) = call(
        last_kernel, [flags, donors] + ghost_tables + states, [((FIELDS, CT, CP), f32)], work, flags=True
    )
    return result.reshape(state.shape)


def solution(mesh):
    fine = Mesh(mesh.devices.reshape(tuple(SIZES[a] for a in AXES)), AXES)
    return jax.shard_map(
        on_device,
        mesh=fine,
        in_specs=(
            P("panel", None, None, LAT, LON),
            P("panel", LAT, LON, None),
            P("panel", None, LAT, LON, None),
            P(None, None, LON),
            P(None, None, LAT),
            P(None, None, LON),
            P(None, None, LAT),
        ),
        out_specs=P("panel", None, None, LAT, LON),
        check_vma=False,
    )
```

```python
import functools
import math

import jax
import jax.numpy as jnp
from jax import lax
from jax.experimental import pallas as pl
from jax.experimental.pallas import tpu as pltpu
from jax.sharding import Mesh, PartitionSpec as P

time_step = 0.25
viscosity = 0.1
resistivity = 0.08
conduction = 0.12
buoyancy = 0.5
gradient = 0.5

AXES = ("panel", "z", "core", "y", "xh")
SIZES = dict(zip(AXES, (2, 8, 2, 4, 2)))
LAT = ("z", "core")
LON = ("y", "xh")

FIELDS = 14
CT = 24
CP = 576
ROWS = 32
COLS = 640
HALO = 4
SLOTS = 48
NT = 384
LANES = 128
TILES = 128
LANE_TILES = COLS // LANES
LAST = COLS - LANES
VMEM_LIMIT = 24 * 1024 * 1024


def lane_of(shape):
    return lax.broadcasted_iota(jnp.int32, shape, len(shape) - 1)


def row_of(shape):
    return lax.broadcasted_iota(jnp.int32, shape, len(shape) - 2)


def lane_gather(block, index):
    return jnp.take_along_axis(block, index, axis=1, mode="promise_in_bounds")


def build_packet(block_of, index_ref, weight_ref):
    totals = [None] * FIELDS
    for t in range(LANE_TILES):
        index = index_ref[t]
        for rb in range(CT // 8):
            weight = weight_ref[rb * LANE_TILES + t]
            for f in range(FIELDS):
                term = weight * lane_gather(block_of(f, rb, t), index)
                totals[f] = term if totals[f] is None else totals[f] + term
    rows = [jnp.sum(total, axis=0, keepdims=True) for total in totals]
    rows += [jnp.zeros((1, LANES), jnp.float32)] * (16 - FIELDS)
    packet = jnp.concatenate(rows, axis=0)
    return packet + pltpu.roll(packet, 64, 1)


def state_block(state_ref, f, rb, t):
    rows = slice(rb * 8, rb * 8 + 8)
    if t < LANE_TILES - 1:
        return state_ref[f, rows, t * LANES : (t + 1) * LANES]
    half = state_ref[f, rows, LAST:CP]
    return jnp.concatenate([half, jnp.zeros((8, LANES - 64), jnp.float32)], axis=1)


def place_of(aux_ref):
    return aux_ref[7, 0].astype(jnp.int32), aux_ref[7, LANES].astype(jnp.int32)


def open_kernel(
    flags_ref, state_hbm, cell_hbm, frac_hbm, ns_source_hbm, we_source_hbm, ns_turn_hbm, we_turn_hbm,
    state_ref, aux_ref, packet_ref, inner_ref, cross_ref, index_ref, weight_ref,
    cell_ref, frac_ref, ns_source_ref, we_source_ref, ns_turn_ref, we_turn_ref, semaphores,
):
    sources = (cell_hbm, frac_hbm, ns_source_hbm, we_source_hbm, ns_turn_hbm, we_turn_hbm, state_hbm)
    targets = (cell_ref, frac_ref, ns_source_ref, we_source_ref, ns_turn_ref, we_turn_ref, state_ref)
    copies = [pltpu.make_async_copy(sources[i], targets[i], semaphores.at[i]) for i in range(len(sources))]
    for copy in copies:
        copy.start()
    for copy in copies[:-1]:
        copy.wait()
    panel = flags_ref[2, 0]
    far_south = flags_ref[0, 0] == NT // CT - 1
    far_east = flags_ref[1, 0] == 7
    aux_ref[...] = jnp.zeros((8, COLS), jnp.float32)
    for i, (table, far) in enumerate(
        ((ns_source_ref, far_south), (ns_turn_ref, far_south), (we_source_ref, far_east), (we_turn_ref, far_east))
    ):
        both = table[panel].astype(jnp.float32)
        aux_ref[i : i + 1, 0 : both.shape[1]] = jnp.where(far, both[1:2, :], both[0:1, :])
    aux_ref[7:8, 0:LANES] = flags_ref[0:1, :].astype(jnp.float32)
    aux_ref[7:8, LANES : 2 * LANES] = flags_ref[1:2, :].astype(jnp.float32)
    shape = (8, LANES)
    lane = lane_of(shape)
    row = row_of(shape)
    copies[-1].wait()
    first_core = (flags_ref[0, 0] & 1) == 0
    for c in range(7):
        for t in range(LANE_TILES):
            cols = slice(t * LANES, (t + 1) * LANES)
            top = [state_block(state_ref, 2 * c + k, 0, t) for k in range(2)]
            end = [state_block(state_ref, 2 * c + k, CT // 8 - 1, t) for k in range(2)]
            north = jnp.where(row < HALO, top[0], pltpu.roll(top[1], HALO, 0))
            south = jnp.where(row < HALO, pltpu.roll(end[0], HALO, 0), end[1])
            inner_ref[c, :, cols] = jnp.where(first_core, south, north)
            cross_ref[c, :, cols] = jnp.where(first_core, north, south)

    def doubled(line):
        line = jnp.concatenate([line, jnp.zeros((1, LANES - SLOTS), jnp.float32)], axis=1)
        line = jnp.broadcast_to(line, shape)
        return jnp.where(lane < 64, line, pltpu.roll(line, 64, 1))

    cell = doubled(cell_ref[...].astype(jnp.float32))
    frac_u = doubled(frac_ref[0:1, :])
    frac_v = doubled(frac_ref[1:2, :])
    lat_off = jnp.floor((cell + 0.5) * (1.0 / (CP - 1)))
    lon_off = cell - lat_off * (CP - 1)
    lat_off = lat_off.astype(jnp.int32)
    second = lane >= 64
    column = lon_off.astype(jnp.int32) + second.astype(jnp.int32)
    used = (lane & 63) < SLOTS
    along = jnp.where(second, frac_v, 1.0 - frac_v)
    for t in range(LANE_TILES):
        local = column - t * LANES
        inside = used & (local >= 0) & (local < LANES)
        index_ref[t] = jnp.where(inside, local, 0)
        for rb in range(CT // 8):
            here = row + rb * 8
            down = jnp.where(here == lat_off, 1.0 - frac_u, jnp.where(here == lat_off + 1, frac_u, 0.0))
            weight_ref[rb * LANE_TILES + t] = jnp.where(inside, down * along, 0.0)
    packet_ref[...] = build_packet(functools.partial(state_block, state_ref), index_ref, weight_ref)

    inner_ref[7] = aux_ref[...]
    cross_ref[7] = aux_ref[...]


def ordered(flag, inner, cross):
    first = (flag & 1) == 0
    return jnp.where(first, inner, cross), jnp.where(first, cross, inner)


def outer_rows(from_south, from_north, k, row):
    if k == 0:
        return jnp.where(row < HALO, from_south, pltpu.roll(from_north, HALO, 0))
    return jnp.where(row < HALO, pltpu.roll(from_south, HALO, 0), from_north)


def side_kernel(aux_ref, state_ref, lat_inner_ref, lat_cross_ref, inner_ref, cross_ref):
    shape = (8, LANES)
    lat, lon = place_of(aux_ref)
    lane = lane_of(shape)
    row = row_of(shape)
    for rb in range(ROWS // 8):
        west = jnp.zeros(shape, jnp.float32)
        east = jnp.zeros(shape, jnp.float32)
        for f in range(FIELDS):
            c, k = f // 2, f % 2
            if rb < CT // 8:
                first = state_block(state_ref, f, rb, 0)
                last = state_block(state_ref, f, rb, LANE_TILES - 1)
            else:
                first = outer_rows(*ordered(lat, lat_inner_ref[c, :, 0:LANES], lat_cross_ref[c, :, 0:LANES]), k, row)
                last = outer_rows(*ordered(lat, lat_inner_ref[c, :, LAST:COLS], lat_cross_ref[c, :, LAST:COLS]), k, row)
            here = (lane >= 8 * f) & (lane < 8 * f + HALO)
            west = jnp.where(here, pltpu.roll(first, 8 * f, 1) if f else first, west)
            east = jnp.where(here, pltpu.roll(last, (8 * f - 60) % LANES, 1), east)
        if rb == 0:
            here = (lane >= 112) & (lane < 112 + HALO)
            west = jnp.where(here, pltpu.roll(aux_ref[:, 0:LANES], 112, 1), west)
            east = jnp.where(here, pltpu.roll(aux_ref[:, LAST:COLS], 112 - 60, 1), east)
        inner, cross = ordered(lon, east, west)
        inner_ref[rb * 8 : rb * 8 + 8, :] = inner
        cross_ref[rb * 8 : rb * 8 + 8, :] = cross


def with_columns(block, from_east, from_west, f, lane):
    block = jnp.where((lane >= 64) & (lane < 64 + HALO), pltpu.roll(from_east, (64 - 8 * f) % LANES, 1), block)
    return jnp.where(lane >= LANES - HALO, pltpu.roll(from_west, (124 - 8 * f) % LANES, 1), block)


def frame_kernel(
    aux_ref, state_ref, lat_inner_ref, lat_cross_ref, lon_inner_ref, lon_cross_ref,
    full_ref, slot_ref, tile_ref, cos_ref, sin_ref, metric_ref,
):
    shape = (8, LANES)
    lat, lon = place_of(aux_ref)
    lane = lane_of(shape)
    row = row_of(shape)
    for rb in range(ROWS // 8):
        rows = slice(rb * 8, rb * 8 + 8)
        east, west = ordered(lon, lon_inner_ref[rows, :], lon_cross_ref[rows, :])
        for f in range(FIELDS):
            c, k = f // 2, f % 2
            for t in range(LANE_TILES):
                cols = slice(t * LANES, (t + 1) * LANES)
                if rb < CT // 8:
                    block = state_block(state_ref, f, rb, t)
                else:
                    south, north = ordered(lat, lat_inner_ref[c, :, cols], lat_cross_ref[c, :, cols])
                    block = outer_rows(south, north, k, row)
                if t == LANE_TILES - 1:
                    block = with_columns(block, east, west, f, lane)
                full_ref[f, rows, cols] = block
    for t in range(LANE_TILES + 1):
        if t < LANE_TILES:
            block = aux_ref[:, t * LANES : (t + 1) * LANES]
            if t == LANE_TILES - 1:
                east, west = ordered(lon, lon_inner_ref[0:8, :], lon_cross_ref[0:8, :])
                block = jnp.where((lane >= 64) & (lane < 64 + HALO), pltpu.roll(east, (64 - 112) % LANES, 1), block)
                block = jnp.where(lane >= LANES - HALO, pltpu.roll(west, 124 - 112, 1), block)
            source = jnp.broadcast_to(block[0:1, :], shape)
            angle = jnp.broadcast_to(block[1:2, :], shape)
        else:
            block = aux_ref[:, 0:LANES]
            south, north = ordered(lat, lat_inner_ref[7, :, 0:LANES], lat_cross_ref[7, :, 0:LANES])
            block = jnp.where((lane >= CT) & (lane < CT + HALO), pltpu.roll(south, CT, 1), block)
            block = jnp.where((lane >= 28) & (lane < 32), pltpu.roll(north, 8, 1), block)
            source = jnp.broadcast_to(block[2:3, :], shape)
            angle = jnp.broadcast_to(block[3:4, :], shape)
        whole = jnp.floor((source + 0.5) * (1.0 / SLOTS))
        tile = whole.astype(jnp.int32)
        slot_ref[t] = (source - whole * SLOTS).astype(jnp.int32) + 64 * (tile & 1)
        tile_ref[t] = tile // 2
        cos_ref[t] = jnp.cos(angle)
        sin_ref[t] = jnp.sin(angle)
    line = row_of((ROWS, LANES))
    line = jnp.where(line >= ROWS - HALO, line - ROWS, line) + lat * CT
    theta = math.pi / 4 + (line.astype(jnp.float32) + 0.5) * ((math.pi / 2) / NT)
    metric_ref[...] = 1.0 / jnp.sin(theta)


def pick_ghosts(donor_ref, slot_ref, tile_ref, cos_ref, sin_ref):
    shape = (8, LANES)
    row = row_of(shape)
    count = LANE_TILES + 1
    low, high = [], []
    for t in range(count):
        slots, pairs = slot_ref[t], tile_ref[t]
        for half, out in ((0, low), (1, high)):
            total = jnp.zeros(shape, jnp.float32)
            for v in range(TILES // 2):
                z, core, y = v // 8, v // 4 % 2, v % 4
                block = donor_ref[core, z * 4 + y, half * 8 : half * 8 + 8, :]
                total = jnp.where(pairs == v, lane_gather(block, slots), total)
            out.append(total)
    ghosts = []
    for t in range(count):
        cosine, sine = cos_ref[t], sin_ref[t]
        first = (row == 2) | (row == 3)
        other = (row == 4) | (row == 5)
        mate = jnp.where(first, pltpu.roll(low[t], 6, 0), pltpu.roll(low[t], 2, 0))
        turn = jnp.where(first, -sine, sine)
        a = jnp.where(first | other, cosine * low[t] + turn * mate, low[t])
        first = row < 2
        mate = jnp.where(first, pltpu.roll(high[t], 6, 0), pltpu.roll(high[t], 2, 0))
        turn = jnp.where(first, -sine, sine)
        b = jnp.where(row < 4, cosine * high[t] + turn * mate, high[t])
        ghosts.append((a, b))
    return ghosts


def keep_ghosts(lon, ghosts, line_ref, column_ref):
    for t in range(LANE_TILES):
        cols = slice(t * LANES, (t + 1) * LANES)
        line_ref[0:8, cols], line_ref[8:16, cols] = ghosts[t]

    def put_column():
        shape = (ROWS, LANES)
        diagonal = lane_of(shape) == row_of(shape)
        for f in range(FIELDS):
            values = jnp.broadcast_to(ghosts[LANE_TILES][f // 8][f % 8 : f % 8 + 1, :], shape)
            column = jnp.sum(jnp.where(diagonal, values, 0.0), axis=1, keepdims=True)
            column_ref[f] = jnp.broadcast_to(column, shape)

    pl.when((lon == 0) | (lon == 7))(put_column)


def tendency(work_ref, metric_ref, rb, k, emit, tile=None, ghosts=None):
    low = rb * 8
    rows = slice(low, low + 8)
    whole = tile is None
    cols = slice(0, COLS) if whole else slice(tile * LANES, (tile + 1) * LANES)
    shape = (8, cols.stop - cols.start)
    row = row_of(shape)
    lane = lane_of(shape)
    metric = metric_ref[rows, :]
    if whole:
        metric = jnp.concatenate([metric] * LANE_TILES, axis=1)
    square = metric * metric
    centre_weight = 4.0 + 2.0 * square
    radial = 0.5 if k == 0 else -0.5

    def value(c):
        return work_ref[2 * c + k, rows, cols]

    def beside(f, step):
        start = (tile + step) % LANE_TILES * LANES
        return work_ref[f, rows, start : start + LANES]

    def coefficients(c):
        return radial * value(c), 0.5 * value(c + 1), (0.5 * metric) * value(c + 2)

    flow_by = coefficients(0)
    field_by = coefficients(3)

    def parts(c):
        f = 2 * c + k
        centre = value(c)
        across = work_ref[2 * c + 1 - k, rows, cols]
        before = work_ref[f, (low - 1) % ROWS : (low - 1) % ROWS + 1, cols]
        after = work_ref[f, (low + 8) % ROWS : (low + 8) % ROWS + 1, cols]
        if ghosts is not None:
            (lat, lon), line_ref, column_ref = ghosts
            if rb == 0:
                before = jnp.where(lat == 0, line_ref[f : f + 1, cols], before)
            if rb == CT // 8 - 1:
                after = jnp.where(lat == NT // CT - 1, line_ref[f : f + 1, cols], after)
        north = jnp.where(row == 0, jnp.broadcast_to(before, shape), pltpu.roll(centre, 1, 0))
        south = jnp.where(row == 7, jnp.broadcast_to(after, shape), pltpu.roll(centre, 7, 0))
        west = pltpu.roll(centre, 1, 1)
        east = pltpu.roll(centre, shape[1] - 1, 1)
        if tile == 0:
            west = jnp.where(lane == 0, jnp.where(lon == 0, column_ref[f, rows, :], pltpu.roll(beside(f, -1), 1, 1)), west)
            east = jnp.where(lane == LANES - 1, pltpu.roll(beside(f, 1), LANES - 1, 1), east)
        elif tile is not None:
            west = jnp.where(lane == 0, pltpu.roll(beside(f, -1), 1, 1), west)
            east = jnp.where(lane == LANES - 1, pltpu.roll(beside(f, 1), LANES - 1, 1), east)
            east = jnp.where((lane == CP - LAST - 1) & (lon == 7), column_ref[f, rows, :], east)
        grad_t = south - north
        grad_p = east - west
        laplace = across + (south + north) + square * (east + west) - centre_weight * centre
        return across, grad_t, grad_p, laplace

    def along(by, p):
        return by[0] * p[0] + by[1] * p[1] + by[2] * p[2]

    for c in range(3):
        p = parts(c)
        u_flow, u_field, u_laplace = along(flow_by, p), along(field_by, p), p[3]
        p = parts(c + 3)
        velocity = along(field_by, p) - u_flow + viscosity * u_laplace
        if c == 0:
            velocity = velocity + buoyancy * value(6)
        emit(c, velocity)
        emit(c + 3, u_field - along(flow_by, p) + resistivity * p[3])
    p = parts(6)
    emit(6, conduction * p[3] - along(flow_by, p) + gradient * value(0))


def inner_kernel(factor, metric_ref, *refs):
    full_ref, now_ref, next_ref = refs if len(refs) == 3 else (refs[0], refs[0], refs[1])
    for rb in range(ROWS // 8):
        rows = slice(rb * 8, rb * 8 + 8)
        for k in range(2):

            def emit(c, value):
                next_ref[2 * c + k, rows, :] = full_ref[2 * c + k, rows, :] + factor * value

            tendency(now_ref, metric_ref, rb, k, emit)


def redo_rim(place, now_ref, metric_ref, line_ref, column_ref, blocks, store):
    lat, lon = place

    def redo(rbs, tile):
        cols = slice(0, COLS) if tile is None else slice(tile * LANES, (tile + 1) * LANES)
        for rb in rbs:
            for k in range(2):

                def emit(c, value):
                    store(2 * c + k, slice(rb * 8, rb * 8 + 8), cols, value)

                tendency(now_ref, metric_ref, rb, k, emit, tile, (place, line_ref, column_ref))

    pl.when(lat == 0)(lambda: redo([0], None))
    pl.when(lat == NT // CT - 1)(lambda: redo([CT // 8 - 1], None))
    pl.when(lon == 0)(lambda: redo(range(blocks), 0))
    pl.when(lon == 7)(lambda: redo(range(blocks), LANE_TILES - 1))


def rim_kernel(
    factor, aux_ref, donor_ref, slot_ref, tile_ref, cos_ref, sin_ref, metric_ref, index_ref, weight_ref, *refs
):
    full_ref, now_ref, inner_ref, next_ref, packet_ref, line_ref, column_ref = refs if len(refs) == 7 else refs[:1] + refs
    place = place_of(aux_ref)
    keep_ghosts(place[1], pick_ghosts(donor_ref, slot_ref, tile_ref, cos_ref, sin_ref), line_ref, column_ref)
    next_ref[...] = inner_ref[...]

    def store(f, rows, cols, value):
        next_ref[f, rows, cols] = full_ref[f, rows, cols] + factor * value

    redo_rim(place, now_ref, metric_ref, line_ref, column_ref, ROWS // 8, store)

    def block_of(f, rb, t):
        return next_ref[f, rb * 8 : rb * 8 + 8, t * LANES : (t + 1) * LANES]

    packet_ref[...] = build_packet(block_of, index_ref, weight_ref)


def last_inner_kernel(metric_ref, full_ref, second_ref, third_ref, fourth_ref, base_ref, out_ref):
    for rb in range(CT // 8):
        rows = slice(rb * 8, rb * 8 + 8)
        for k in range(2):

            def emit(c, value):
                f = 2 * c + k
                base = second_ref[f, rows, :] + 2.0 * third_ref[f, rows, :] + fourth_ref[f, rows, :] - full_ref[f, rows, :]
                base = (1.0 / 3.0) * base
                base_ref[f, rows, :] = base
                out_ref[f, rows, :] = base + (time_step / 6) * value

            tendency(fourth_ref, metric_ref, rb, k, emit)


def last_rim_kernel(
    aux_ref, donor_ref, slot_ref, tile_ref, cos_ref, sin_ref, metric_ref, base_ref, inner_ref, now_ref,
    out_ref, line_ref, column_ref,
):
    place = place_of(aux_ref)
    keep_ghosts(place[1], pick_ghosts(donor_ref, slot_ref, tile_ref, cos_ref, sin_ref), line_ref, column_ref)
    for f in range(FIELDS):
        out_ref[f] = inner_ref[f, :, 0:CP]

    def store(f, rows, cols, value):
        cols = slice(cols.start, min(cols.stop, CP))
        out = base_ref[f, rows, cols] + (time_step / 6) * value[:, : cols.stop - cols.start]
        out_ref[f, rows, cols] = out

    redo_rim(place, now_ref, metric_ref, line_ref, column_ref, CT // 8, store)


def call(kernel, ins, outs, scratch=(), cost=0, left=()):
    vmem = pl.BlockSpec(memory_space=pltpu.VMEM)
    hbm = pl.BlockSpec(memory_space=pltpu.HBM)
    shapes = tuple(jax.ShapeDtypeStruct(s, d) for s, d in outs)
    ins = [pltpu.with_memory_space_constraint(a, pltpu.HBM) if i in left else a for i, a in enumerate(ins)]
    return pl.pallas_call(
        kernel,
        out_shape=shapes,
        in_specs=[hbm if i in left else vmem for i in range(len(ins))],
        out_specs=(vmem,) * len(outs),
        scratch_shapes=list(scratch),
        compiler_params=pltpu.CompilerParams(vmem_limit_bytes=VMEM_LIMIT),
        cost_estimate=pl.CostEstimate(flops=cost * 1000, bytes_accessed=cost, transcendentals=0) if cost else None,
    )(*ins)


def coordinates(axes):
    points = [()]
    for a in axes:
        points = [q + (i,) for q in points for i in range(SIZES[a])]
    return points


def permute(value, axes, move):
    points = coordinates(axes)
    place = {q: i for i, q in enumerate(points)}
    pairs = []
    for q in points:
        to = move(q)
        if to is not None:
            pairs.append((place[q], place[to]))
    return lax.ppermute(value, axes if len(axes) > 1 else axes[0], pairs)


def within(value, axes):
    return permute(value, axes, lambda q: (q[0], 1 - q[1]))


def between(value, axes):
    count = SIZES[axes[0]]
    return permute(value, axes, lambda q: ((q[0] + 1) % count, 0) if q[1] == 1 else ((q[0] - 1) % count, 1))


def swap_packets(packet):
    same = permute(packet, ("panel", "xh"), lambda q: (1 - q[0], q[1]))
    other = permute(packet, ("panel", "xh"), lambda q: (1 - q[0], 1 - q[1]))
    second = lane_of(packet.shape) >= 64
    return jnp.where(second == (lax.axis_index("xh") == 1), same, other)


def spread_packets(pair, inner):
    if inner is not None:
        pair, _ = lax.optimization_barrier((pair, inner))
    count = SIZES["z"] * SIZES["y"]
    spread = lax.all_to_all(jnp.broadcast_to(pair[None], (count,) + pair.shape), ("z", "y"), 0, 0)
    return lax.all_gather(spread, "core")


def on_device(state, pack_cell, pack_frac, ns_source, we_source, ns_turn, we_turn):
    f32 = jnp.float32
    tile = state.reshape(FIELDS, CT, CP)
    lat = lax.axis_index(LAT)
    lon = lax.axis_index(LON)
    panel = lax.axis_index("panel")
    flags = jnp.broadcast_to(jnp.stack([lat, lon, panel] + [panel] * 5).astype(jnp.int32)[:, None], (8, LANES))
    raw = [pack_cell.reshape(1, SLOTS), pack_frac.reshape(2, SLOTS), ns_source, we_source, ns_turn, we_turn]
    vreg = (8, LANES)
    packed = ((16, LANES), f32)
    whole = ((FIELDS, ROWS, COLS), f32)
    message = ((8, 8, COLS), f32)
    side = ((ROWS, LANES), f32)
    tile, aux, packet, lat_inner, lat_cross, index, weight = call(
        open_kernel,
        [flags, tile] + raw,
        [
            ((FIELDS, CT, CP), f32),
            ((8, COLS), f32),
            packed,
            message,
            message,
            ((LANE_TILES,) + vreg, jnp.int32),
            ((3 * LANE_TILES,) + vreg, f32),
        ],
        scratch=[pltpu.VMEM(a.shape, a.dtype) for a in raw] + [pltpu.SemaphoreType.DMA((len(raw) + 1,))],
        left=range(1, 8),
    )
    lat_inner = within(lat_inner, LAT)
    lat_cross = between(lat_cross, LAT)
    lon_inner, lon_cross = call(side_kernel, [aux, tile, lat_inner, lat_cross], [side, side])
    pair, _ = lax.optimization_barrier((swap_packets(packet), lon_inner))
    lon_inner = within(lon_inner, LON)
    lon_cross = between(lon_cross, LON)
    points = (LANE_TILES + 1,) + vreg
    full, slot, where, cosine, sine, metric = call(
        frame_kernel,
        [aux, tile, lat_inner, lat_cross, lon_inner, lon_cross],
        [whole, (points, jnp.int32), (points, jnp.int32), (points, f32), (points, f32), ((ROWS, LANES), f32)],
    )
    tables = [slot, where, cosine, sine, metric]
    kept = [pltpu.VMEM((16, COLS), f32), pltpu.VMEM((FIELDS, ROWS, LANES), f32)]
    states = [full]
    for factor in (time_step / 2, time_step / 2, time_step):
        if len(states) > 1:
            pair = swap_packets(packet)
        now = [states[-1]] if len(states) > 1 else []
        (inner,) = call(functools.partial(inner_kernel, factor), [metric, full] + now, [whole], cost=2_000_000 if now else 50_000_000)
        after, packet = call(
            functools.partial(rim_kernel, factor),
            [aux, spread_packets(pair, inner if now else None)] + tables + [index, weight, full] + now + [inner],
            [whole, packed],
                scratch=kept,
        )
        states.append(after)
    pair = swap_packets(packet)
    inner_shape = ((FIELDS, CT, COLS), f32)
    base, inner = call(last_inner_kernel, [metric] + states, [inner_shape, inner_shape], cost=2_000_000)
    (result,) = call(
        last_rim_kernel,
        [aux, spread_packets(pair, inner)] + tables + [base, inner, states[-1]],
        [((FIELDS, CT, CP), f32)],
        scratch=kept,
    )
    return result.reshape(state.shape)


def solution(mesh):
    fine = Mesh(mesh.devices.reshape(tuple(SIZES[a] for a in AXES)), AXES)
    return jax.shard_map(
        on_device,
        mesh=fine,
        in_specs=(
            P("panel", None, None, LAT, LON),
            P("panel", LAT, LON, None),
            P("panel", None, LAT, LON, None),
            P(None, None, LON),
            P(None, None, LAT),
            P(None, None, LON),
            P(None, None, LAT),
        ),
        out_specs=P("panel", None, None, LAT, LON),
        check_vma=False,
    )
```

```python
import functools
import math

import jax
import jax.numpy as jnp
from jax import lax
from jax.experimental import pallas as pl
from jax.experimental.pallas import tpu as pltpu
from jax.sharding import Mesh, PartitionSpec as P

time_step = 0.25
viscosity = 0.1
resistivity = 0.08
conduction = 0.12
buoyancy = 0.5
gradient = 0.5

AXES = ("panel", "z", "core", "y", "xh")
SIZES = dict(zip(AXES, (2, 8, 2, 4, 2)))
LAT = ("z", "core")
LON = ("y", "xh")

FIELDS = 14
CT = 24
CP = 576
ROWS = 32
COLS = 640
HALO = 4
SLOTS = 48
NT = 384
LANES = 128
TILES = 128
LANE_TILES = COLS // LANES
LAST = COLS - LANES
VMEM_LIMIT = 24 * 1024 * 1024


def lane_of(shape):
    return lax.broadcasted_iota(jnp.int32, shape, len(shape) - 1)


def row_of(shape):
    return lax.broadcasted_iota(jnp.int32, shape, len(shape) - 2)


def lane_gather(block, index):
    return jnp.take_along_axis(block, index, axis=1, mode="promise_in_bounds")


def build_packet(block_of, index_ref, weight_ref):
    totals = [None] * FIELDS
    for t in range(LANE_TILES):
        index = index_ref[t]
        for rb in range(CT // 8):
            weight = weight_ref[rb * LANE_TILES + t]
            for f in range(FIELDS):
                term = weight * lane_gather(block_of(f, rb, t), index)
                totals[f] = term if totals[f] is None else totals[f] + term
    rows = [jnp.sum(total, axis=0, keepdims=True) for total in totals]
    rows += [jnp.zeros((1, LANES), jnp.float32)] * (16 - FIELDS)
    packet = jnp.concatenate(rows, axis=0)
    return packet + pltpu.roll(packet, 64, 1)


def state_block(state_ref, f, rb, t):
    rows = slice(rb * 8, rb * 8 + 8)
    if t < LANE_TILES - 1:
        return state_ref[f, rows, t * LANES : (t + 1) * LANES]
    half = state_ref[f, rows, LAST:CP]
    return jnp.concatenate([half, jnp.zeros((8, LANES - 64), jnp.float32)], axis=1)


def place_of(aux_ref):
    return aux_ref[7, 0].astype(jnp.int32), aux_ref[7, LANES].astype(jnp.int32)


def open_kernel(
    flags_ref, state_hbm, cell_hbm, frac_hbm, ns_source_hbm, we_source_hbm, ns_turn_hbm, we_turn_hbm,
    state_ref, aux_ref, packet_ref, inner_ref, cross_ref, index_ref, weight_ref,
    cell_ref, frac_ref, ns_source_ref, we_source_ref, ns_turn_ref, we_turn_ref, semaphores,
):
    sources = (cell_hbm, frac_hbm, ns_source_hbm, we_source_hbm, ns_turn_hbm, we_turn_hbm, state_hbm)
    targets = (cell_ref, frac_ref, ns_source_ref, we_source_ref, ns_turn_ref, we_turn_ref, state_ref)
    copies = [pltpu.make_async_copy(sources[i], targets[i], semaphores.at[i]) for i in range(len(sources))]
    for copy in copies:
        copy.start()
    for copy in copies[:-1]:
        copy.wait()
    panel = flags_ref[2, 0]
    far_south = flags_ref[0, 0] >= NT // CT - 2
    far_east = flags_ref[1, 0] == 7
    aux_ref[...] = jnp.zeros((8, COLS), jnp.float32)
    for i, (table, far) in enumerate(
        ((ns_source_ref, far_south), (ns_turn_ref, far_south), (we_source_ref, far_east), (we_turn_ref, far_east))
    ):
        both = table[panel].astype(jnp.float32)
        aux_ref[i : i + 1, 0 : both.shape[1]] = jnp.where(far, both[1:2, :], both[0:1, :])
    aux_ref[7:8, 0:LANES] = flags_ref[0:1, :].astype(jnp.float32)
    aux_ref[7:8, LANES : 2 * LANES] = flags_ref[1:2, :].astype(jnp.float32)
    shape = (8, LANES)
    lane = lane_of(shape)
    row = row_of(shape)
    copies[-1].wait()
    first_core = (flags_ref[0, 0] & 1) == 0
    for c in range(7):
        for t in range(LANE_TILES):
            cols = slice(t * LANES, (t + 1) * LANES)
            top = [state_block(state_ref, 2 * c + k, 0, t) for k in range(2)]
            end = [state_block(state_ref, 2 * c + k, CT // 8 - 1, t) for k in range(2)]
            north = jnp.where(row < HALO, top[0], pltpu.roll(top[1], HALO, 0))
            south = jnp.where(row < HALO, pltpu.roll(end[0], HALO, 0), end[1])
            inner_ref[c, :, cols] = jnp.where(first_core, south, north)
            cross_ref[c, :, cols] = jnp.where(first_core, north, south)

    def doubled(line):
        line = jnp.concatenate([line, jnp.zeros((1, LANES - SLOTS), jnp.float32)], axis=1)
        line = jnp.broadcast_to(line, shape)
        return jnp.where(lane < 64, line, pltpu.roll(line, 64, 1))

    cell = doubled(cell_ref[...].astype(jnp.float32))
    frac_u = doubled(frac_ref[0:1, :])
    frac_v = doubled(frac_ref[1:2, :])
    lat_off = jnp.floor((cell + 0.5) * (1.0 / (CP - 1)))
    lon_off = cell - lat_off * (CP - 1)
    lat_off = lat_off.astype(jnp.int32)
    second = lane >= 64
    column = lon_off.astype(jnp.int32) + second.astype(jnp.int32)
    used = (lane & 63) < SLOTS
    along = jnp.where(second, frac_v, 1.0 - frac_v)
    for t in range(LANE_TILES):
        local = column - t * LANES
        inside = used & (local >= 0) & (local < LANES)
        index_ref[t] = jnp.where(inside, local, 0)
        for rb in range(CT // 8):
            here = row + rb * 8
            down = jnp.where(here == lat_off, 1.0 - frac_u, jnp.where(here == lat_off + 1, frac_u, 0.0))
            weight_ref[rb * LANE_TILES + t] = jnp.where(inside, down * along, 0.0)
    packet_ref[...] = build_packet(functools.partial(state_block, state_ref), index_ref, weight_ref)

    inner_ref[7] = aux_ref[...]
    cross_ref[7] = aux_ref[...]


def ordered(flag, inner, cross):
    first = (flag & 1) == 0
    return jnp.where(first, inner, cross), jnp.where(first, cross, inner)


def outer_rows(from_south, from_north, k, row):
    if k == 0:
        return jnp.where(row < HALO, from_south, pltpu.roll(from_north, HALO, 0))
    return jnp.where(row < HALO, pltpu.roll(from_south, HALO, 0), from_north)


def column_list(aux_ref, lat_inner_ref, lat_cross_ref):
    lane = lane_of((8, LANES))
    block = aux_ref[:, 0:LANES]
    south, north = ordered(place_of(aux_ref)[0], lat_inner_ref[7, :, 0:LANES], lat_cross_ref[7, :, 0:LANES])
    block = jnp.where((lane >= CT) & (lane < CT + HALO), pltpu.roll(south, CT, 1), block)
    return jnp.where((lane >= ROWS - HALO) & (lane < ROWS), pltpu.roll(north, 8, 1), block)


def donor_places(source):
    whole = jnp.floor((source + 0.5) * (1.0 / SLOTS))
    tile = whole.astype(jnp.int32)
    return (source - whole * SLOTS).astype(jnp.int32) + 64 * (tile & 1), tile // 2


def side_kernel(aux_ref, state_ref, lat_inner_ref, lat_cross_ref, inner_ref, cross_ref, column_ref):
    shape = (8, LANES)
    source = jnp.broadcast_to(column_list(aux_ref, lat_inner_ref, lat_cross_ref)[2:3, :], shape)
    column_ref[0:8, :], column_ref[8:16, :] = donor_places(source)
    lat, lon = place_of(aux_ref)
    lane = lane_of(shape)
    row = row_of(shape)
    for rb in range(ROWS // 8):
        west = jnp.zeros(shape, jnp.float32)
        east = jnp.zeros(shape, jnp.float32)
        for f in range(FIELDS):
            c, k = f // 2, f % 2
            if rb < CT // 8:
                first = state_block(state_ref, f, rb, 0)
                last = state_block(state_ref, f, rb, LANE_TILES - 1)
            else:
                first = outer_rows(*ordered(lat, lat_inner_ref[c, :, 0:LANES], lat_cross_ref[c, :, 0:LANES]), k, row)
                last = outer_rows(*ordered(lat, lat_inner_ref[c, :, LAST:COLS], lat_cross_ref[c, :, LAST:COLS]), k, row)
            here = (lane >= 8 * f) & (lane < 8 * f + HALO)
            west = jnp.where(here, pltpu.roll(first, 8 * f, 1) if f else first, west)
            east = jnp.where(here, pltpu.roll(last, (8 * f - 60) % LANES, 1), east)
        if rb == 0:
            here = (lane >= 112) & (lane < 112 + HALO)
            west = jnp.where(here, pltpu.roll(aux_ref[:, 0:LANES], 112, 1), west)
            east = jnp.where(here, pltpu.roll(aux_ref[:, LAST:COLS], 112 - 60, 1), east)
        inner, cross = ordered(lon, east, west)
        inner_ref[rb * 8 : rb * 8 + 8, :] = inner
        cross_ref[rb * 8 : rb * 8 + 8, :] = cross


def with_columns(block, from_east, from_west, f, lane):
    block = jnp.where((lane >= 64) & (lane < 64 + HALO), pltpu.roll(from_east, (64 - 8 * f) % LANES, 1), block)
    return jnp.where(lane >= LANES - HALO, pltpu.roll(from_west, (124 - 8 * f) % LANES, 1), block)


def frame_kernel(
    aux_ref, state_ref, lat_inner_ref, lat_cross_ref, lon_inner_ref, lon_cross_ref,
    full_ref, slot_ref, tile_ref, cos_ref, sin_ref, metric_ref,
):
    shape = (8, LANES)
    lat, lon = place_of(aux_ref)
    lane = lane_of(shape)
    row = row_of(shape)
    for rb in range(ROWS // 8):
        rows = slice(rb * 8, rb * 8 + 8)
        east, west = ordered(lon, lon_inner_ref[rows, :], lon_cross_ref[rows, :])
        for f in range(FIELDS):
            c, k = f // 2, f % 2
            for t in range(LANE_TILES):
                cols = slice(t * LANES, (t + 1) * LANES)
                if rb < CT // 8:
                    block = state_block(state_ref, f, rb, t)
                else:
                    south, north = ordered(lat, lat_inner_ref[c, :, cols], lat_cross_ref[c, :, cols])
                    block = outer_rows(south, north, k, row)
                if t == LANE_TILES - 1:
                    block = with_columns(block, east, west, f, lane)
                full_ref[f, rows, cols] = block
    for t in range(LANE_TILES + 1):
        if t < LANE_TILES:
            block = aux_ref[:, t * LANES : (t + 1) * LANES]
            if t == LANE_TILES - 1:
                east, west = ordered(lon, lon_inner_ref[0:8, :], lon_cross_ref[0:8, :])
                block = jnp.where((lane >= 64) & (lane < 64 + HALO), pltpu.roll(east, (64 - 112) % LANES, 1), block)
                block = jnp.where(lane >= LANES - HALO, pltpu.roll(west, 124 - 112, 1), block)
            source = jnp.broadcast_to(block[0:1, :], shape)
            angle = jnp.broadcast_to(block[1:2, :], shape)
        else:
            block = column_list(aux_ref, lat_inner_ref, lat_cross_ref)
            source = jnp.broadcast_to(block[2:3, :], shape)
            angle = jnp.broadcast_to(block[3:4, :], shape)
        slot_ref[t], tile_ref[t] = donor_places(source)
        cos_ref[t] = jnp.cos(angle)
        sin_ref[t] = jnp.sin(angle)
    line = row_of((ROWS, LANES))
    line = jnp.where(line >= ROWS - HALO, line - ROWS, line) + lat * CT
    theta = math.pi / 4 + (line.astype(jnp.float32) + 0.5) * ((math.pi / 2) / NT)
    metric_ref[...] = 1.0 / jnp.sin(theta)


def pick_kernel(aux_ref, donor_ref, slot_ref, tile_ref, other_ref, out_ref):
    mine = 4 * (place_of(aux_ref)[0] & 1)
    count = LANE_TILES + 1
    tables = [(slot_ref[t], tile_ref[t]) for t in range(count)] + [(other_ref[0:8, :], other_ref[8:16, :])]
    for t, (slots, pairs) in enumerate(tables):
        pairs = pairs - mine
        for half in range(2):
            rows = slice(half * 8, half * 8 + 8)
            total = jnp.zeros((8, LANES), jnp.float32)
            for v in range(TILES // 4):
                block = donor_ref[v, rows, :]
                total = jnp.where(pairs == v // 4 * 8 + v % 4, lane_gather(block, slots), total)
            out_ref[t, rows, :] = total


def turned_ghosts(share_ref, other_ref, cos_ref, sin_ref):
    shape = (8, LANES)
    row = row_of(shape)
    count = LANE_TILES + 1
    low, high = [], []
    for t in range(count):
        theirs = t if t < LANE_TILES else count
        for out, rows in ((low, slice(0, 8)), (high, slice(8, 16))):
            out.append(share_ref[t, rows, :] + other_ref[theirs, rows, :])
    ghosts = []
    for t in range(count):
        cosine, sine = cos_ref[t], sin_ref[t]
        first = (row == 2) | (row == 3)
        other = (row == 4) | (row == 5)
        mate = jnp.where(first, pltpu.roll(low[t], 6, 0), pltpu.roll(low[t], 2, 0))
        turn = jnp.where(first, -sine, sine)
        a = jnp.where(first | other, cosine * low[t] + turn * mate, low[t])
        first = row < 2
        mate = jnp.where(first, pltpu.roll(high[t], 6, 0), pltpu.roll(high[t], 2, 0))
        turn = jnp.where(first, -sine, sine)
        b = jnp.where(row < 4, cosine * high[t] + turn * mate, high[t])
        ghosts.append((a, b))
    return ghosts


def keep_ghosts(lon, ghosts, line_ref, column_ref):
    for t in range(LANE_TILES):
        cols = slice(t * LANES, (t + 1) * LANES)
        line_ref[0:8, cols], line_ref[8:16, cols] = ghosts[t]

    def put_column():
        shape = (ROWS, LANES)
        diagonal = lane_of(shape) == row_of(shape)
        for f in range(FIELDS):
            values = jnp.broadcast_to(ghosts[LANE_TILES][f // 8][f % 8 : f % 8 + 1, :], shape)
            column = jnp.sum(jnp.where(diagonal, values, 0.0), axis=1, keepdims=True)
            column_ref[f] = jnp.broadcast_to(column, shape)

    pl.when((lon == 0) | (lon == 7))(put_column)


def tendency(work_ref, metric_ref, rb, k, emit, tile=None, ghosts=None):
    low = rb * 8
    rows = slice(low, low + 8)
    whole = tile is None
    cols = slice(0, COLS) if whole else slice(tile * LANES, (tile + 1) * LANES)
    shape = (8, cols.stop - cols.start)
    row = row_of(shape)
    lane = lane_of(shape)
    metric = metric_ref[rows, :]
    if whole:
        metric = jnp.concatenate([metric] * LANE_TILES, axis=1)
    square = metric * metric
    centre_weight = 4.0 + 2.0 * square
    radial = 0.5 if k == 0 else -0.5

    def value(c):
        return work_ref[2 * c + k, rows, cols]

    def beside(f, step):
        start = (tile + step) % LANE_TILES * LANES
        return work_ref[f, rows, start : start + LANES]

    def coefficients(c):
        return radial * value(c), 0.5 * value(c + 1), (0.5 * metric) * value(c + 2)

    flow_by = coefficients(0)
    field_by = coefficients(3)

    def parts(c):
        f = 2 * c + k
        centre = value(c)
        across = work_ref[2 * c + 1 - k, rows, cols]
        before = work_ref[f, (low - 1) % ROWS : (low - 1) % ROWS + 1, cols]
        after = work_ref[f, (low + 8) % ROWS : (low + 8) % ROWS + 1, cols]
        if ghosts is not None:
            (lat, lon), line_ref, column_ref = ghosts
            if rb == 0:
                before = jnp.where(lat == 0, line_ref[f : f + 1, cols], before)
            if rb == CT // 8 - 1:
                after = jnp.where(lat == NT // CT - 1, line_ref[f : f + 1, cols], after)
        north = jnp.where(row == 0, jnp.broadcast_to(before, shape), pltpu.roll(centre, 1, 0))
        south = jnp.where(row == 7, jnp.broadcast_to(after, shape), pltpu.roll(centre, 7, 0))
        west = pltpu.roll(centre, 1, 1)
        east = pltpu.roll(centre, shape[1] - 1, 1)
        if tile == 0:
            west = jnp.where(lane == 0, jnp.where(lon == 0, column_ref[f, rows, :], pltpu.roll(beside(f, -1), 1, 1)), west)
            east = jnp.where(lane == LANES - 1, pltpu.roll(beside(f, 1), LANES - 1, 1), east)
        elif tile is not None:
            west = jnp.where(lane == 0, pltpu.roll(beside(f, -1), 1, 1), west)
            east = jnp.where(lane == LANES - 1, pltpu.roll(beside(f, 1), LANES - 1, 1), east)
            east = jnp.where((lane == CP - LAST - 1) & (lon == 7), column_ref[f, rows, :], east)
        grad_t = south - north
        grad_p = east - west
        laplace = across + (south + north) + square * (east + west) - centre_weight * centre
        return across, grad_t, grad_p, laplace

    def along(by, p):
        return by[0] * p[0] + by[1] * p[1] + by[2] * p[2]

    for c in range(3):
        p = parts(c)
        u_flow, u_field, u_laplace = along(flow_by, p), along(field_by, p), p[3]
        p = parts(c + 3)
        velocity = along(field_by, p) - u_flow + viscosity * u_laplace
        if c == 0:
            velocity = velocity + buoyancy * value(6)
        emit(c, velocity)
        emit(c + 3, u_field - along(flow_by, p) + resistivity * p[3])
    p = parts(6)
    emit(6, conduction * p[3] - along(flow_by, p) + gradient * value(0))


def inner_kernel(factor, metric_ref, *refs):
    full_ref, now_ref, next_ref = refs if len(refs) == 3 else (refs[0], refs[0], refs[1])
    for rb in range(ROWS // 8):
        rows = slice(rb * 8, rb * 8 + 8)
        for k in range(2):

            def emit(c, value):
                next_ref[2 * c + k, rows, :] = full_ref[2 * c + k, rows, :] + factor * value

            tendency(now_ref, metric_ref, rb, k, emit)


def redo_rim(place, now_ref, metric_ref, line_ref, column_ref, blocks, store):
    lat, lon = place

    def redo(rbs, tile):
        cols = slice(0, COLS) if tile is None else slice(tile * LANES, (tile + 1) * LANES)
        for rb in rbs:
            for k in range(2):

                def emit(c, value):
                    store(2 * c + k, slice(rb * 8, rb * 8 + 8), cols, value)

                tendency(now_ref, metric_ref, rb, k, emit, tile, (place, line_ref, column_ref))

    pl.when(lat == 0)(lambda: redo([0], None))
    pl.when(lat == NT // CT - 1)(lambda: redo([CT // 8 - 1], None))
    pl.when(lon == 0)(lambda: redo(range(blocks), 0))
    pl.when(lon == 7)(lambda: redo(range(blocks), LANE_TILES - 1))


def rim_kernel(
    factor, aux_ref, share_ref, other_ref, cos_ref, sin_ref, metric_ref, index_ref, weight_ref, *refs
):
    full_ref, now_ref, inner_ref, next_ref, packet_ref, line_ref, column_ref = refs if len(refs) == 7 else refs[:1] + refs
    place = place_of(aux_ref)
    keep_ghosts(place[1], turned_ghosts(share_ref, other_ref, cos_ref, sin_ref), line_ref, column_ref)
    next_ref[...] = inner_ref[...]

    def store(f, rows, cols, value):
        next_ref[f, rows, cols] = full_ref[f, rows, cols] + factor * value

    redo_rim(place, now_ref, metric_ref, line_ref, column_ref, ROWS // 8, store)

    def block_of(f, rb, t):
        return next_ref[f, rb * 8 : rb * 8 + 8, t * LANES : (t + 1) * LANES]

    packet_ref[...] = build_packet(block_of, index_ref, weight_ref)


def last_inner_kernel(metric_ref, full_ref, second_ref, third_ref, fourth_ref, base_ref, out_ref):
    for rb in range(CT // 8):
        rows = slice(rb * 8, rb * 8 + 8)
        for k in range(2):

            def emit(c, value):
                f = 2 * c + k
                base = second_ref[f, rows, :] + 2.0 * third_ref[f, rows, :] + fourth_ref[f, rows, :] - full_ref[f, rows, :]
                base = (1.0 / 3.0) * base
                base_ref[f, rows, :] = base
                out_ref[f, rows, :] = base + (time_step / 6) * value

            tendency(fourth_ref, metric_ref, rb, k, emit)


def last_rim_kernel(
    aux_ref, share_ref, other_ref, cos_ref, sin_ref, metric_ref, base_ref, inner_ref, now_ref,
    out_ref, line_ref, column_ref,
):
    place = place_of(aux_ref)
    keep_ghosts(place[1], turned_ghosts(share_ref, other_ref, cos_ref, sin_ref), line_ref, column_ref)
    for f in range(FIELDS):
        out_ref[f] = inner_ref[f, :, 0:CP]

    def store(f, rows, cols, value):
        cols = slice(cols.start, min(cols.stop, CP))
        out = base_ref[f, rows, cols] + (time_step / 6) * value[:, : cols.stop - cols.start]
        out_ref[f, rows, cols] = out

    redo_rim(place, now_ref, metric_ref, line_ref, column_ref, CT // 8, store)


def call(kernel, ins, outs, scratch=(), cost=0, left=()):
    vmem = pl.BlockSpec(memory_space=pltpu.VMEM)
    hbm = pl.BlockSpec(memory_space=pltpu.HBM)
    shapes = tuple(jax.ShapeDtypeStruct(s, d) for s, d in outs)
    ins = [pltpu.with_memory_space_constraint(a, pltpu.HBM) if i in left else a for i, a in enumerate(ins)]
    return pl.pallas_call(
        kernel,
        out_shape=shapes,
        in_specs=[hbm if i in left else vmem for i in range(len(ins))],
        out_specs=(vmem,) * len(outs),
        scratch_shapes=list(scratch),
        compiler_params=pltpu.CompilerParams(vmem_limit_bytes=VMEM_LIMIT),
        cost_estimate=pl.CostEstimate(flops=cost * 1000, bytes_accessed=cost, transcendentals=0) if cost else None,
    )(*ins)


def coordinates(axes):
    points = [()]
    for a in axes:
        points = [q + (i,) for q in points for i in range(SIZES[a])]
    return points


def permute(value, axes, move):
    points = coordinates(axes)
    place = {q: i for i, q in enumerate(points)}
    pairs = []
    for q in points:
        to = move(q)
        if to is not None:
            pairs.append((place[q], place[to]))
    return lax.ppermute(value, axes if len(axes) > 1 else axes[0], pairs)


def within(value, axes):
    return permute(value, axes, lambda q: (q[0], 1 - q[1]))


def between(value, axes):
    count = SIZES[axes[0]]
    return permute(value, axes, lambda q: ((q[0] + 1) % count, 0) if q[1] == 1 else ((q[0] - 1) % count, 1))


def swap_packets(packet):
    same = permute(packet, ("panel", "xh"), lambda q: (1 - q[0], q[1]))
    other = permute(packet, ("panel", "xh"), lambda q: (1 - q[0], 1 - q[1]))
    second = lane_of(packet.shape) >= 64
    return jnp.where(second == (lax.axis_index("xh") == 1), same, other)


def spread_packets(pair):
    count = SIZES["z"] * SIZES["y"]
    return lax.all_to_all(jnp.broadcast_to(pair[None], (count,) + pair.shape), ("z", "y"), 0, 0)


def other_core(value):
    return permute(value, ("core",), lambda q: (1 - q[0],))


def on_device(state, pack_cell, pack_frac, ns_source, we_source, ns_turn, we_turn):
    f32 = jnp.float32
    tile = state.reshape(FIELDS, CT, CP)
    lat = lax.axis_index(LAT)
    lon = lax.axis_index(LON)
    panel = lax.axis_index("panel")
    flags = jnp.broadcast_to(jnp.stack([lat, lon, panel] + [panel] * 5).astype(jnp.int32)[:, None], (8, LANES))
    raw = [pack_cell.reshape(1, SLOTS), pack_frac.reshape(2, SLOTS), ns_source, we_source, ns_turn, we_turn]
    vreg = (8, LANES)
    packed = ((16, LANES), f32)
    whole = ((FIELDS, ROWS, COLS), f32)
    message = ((8, 8, COLS), f32)
    side = ((ROWS, LANES), f32)
    tile, aux, packet, lat_inner, lat_cross, index, weight = call(
        open_kernel,
        [flags, tile] + raw,
        [
            ((FIELDS, CT, CP), f32),
            ((8, COLS), f32),
            packed,
            message,
            message,
            ((LANE_TILES,) + vreg, jnp.int32),
            ((3 * LANE_TILES,) + vreg, f32),
        ],
        scratch=[pltpu.VMEM(a.shape, a.dtype) for a in raw] + [pltpu.SemaphoreType.DMA((len(raw) + 1,))],
        left=range(1, 8),
    )
    lat_inner = within(lat_inner, LAT)
    lat_cross = between(lat_cross, LAT)
    lon_inner, lon_cross, column = call(
        side_kernel, [aux, tile, lat_inner, lat_cross], [side, side, ((16, LANES), jnp.int32)], cost=8_000_000
    )
    column = other_core(column)
    pair = swap_packets(packet)
    lon_inner = within(lon_inner, LON)
    lon_cross = between(lon_cross, LON)
    donors = spread_packets(pair)
    donors, lon_inner, lon_cross = lax.optimization_barrier((donors, lon_inner, lon_cross))
    points = (LANE_TILES + 1,) + vreg
    full, slot, where, cosine, sine, metric = call(
        frame_kernel,
        [aux, tile, lat_inner, lat_cross, lon_inner, lon_cross],
        [whole, (points, jnp.int32), (points, jnp.int32), (points, f32), (points, f32), ((ROWS, LANES), f32)],
    )
    lists = [slot, where, column]
    kept = [pltpu.VMEM((16, COLS), f32), pltpu.VMEM((FIELDS, ROWS, LANES), f32)]

    def ghost_tables(donors):
        (share,) = call(pick_kernel, [aux, donors] + lists, [((LANE_TILES + 2, 16, LANES), f32)])
        return [aux, share, other_core(share), cosine, sine, metric]

    states = [full]
    for factor in (time_step / 2, time_step / 2, time_step):
        now = [states[-1]] if len(states) > 1 else []
        if now:
            pair = swap_packets(packet)
        (inner,) = call(functools.partial(inner_kernel, factor), [metric, full] + now, [whole], cost=2_000_000)
        if now:
            pair, inner = lax.optimization_barrier((pair, inner))
            donors = spread_packets(pair)
        after, packet = call(
            functools.partial(rim_kernel, factor),
            ghost_tables(donors) + [index, weight, full] + now + [inner],
            [whole, packed],
            scratch=kept,
        )
        states.append(after)
    pair = swap_packets(packet)
    inner_shape = ((FIELDS, CT, COLS), f32)
    base, inner = call(last_inner_kernel, [metric] + states, [inner_shape, inner_shape], cost=2_000_000)
    pair, inner = lax.optimization_barrier((pair, inner))
    (result,) = call(
        last_rim_kernel,
        ghost_tables(spread_packets(pair)) + [base, inner, states[-1]],
        [((FIELDS, CT, CP), f32)],
        scratch=kept,
    )
    return result.reshape(state.shape)


def solution(mesh):
    fine = Mesh(mesh.devices.reshape(tuple(SIZES[a] for a in AXES)), AXES)
    return jax.shard_map(
        on_device,
        mesh=fine,
        in_specs=(
            P("panel", None, None, LAT, LON),
            P("panel", LAT, LON, None),
            P("panel", None, LAT, LON, None),
            P(None, None, LON),
            P(None, None, LAT),
            P(None, None, LON),
            P(None, None, LAT),
        ),
        out_specs=P("panel", None, None, LAT, LON),
        check_vma=False,
    )
```

```python
import functools
import math

import jax
import jax.numpy as jnp
from jax import lax
from jax.experimental import pallas as pl
from jax.experimental.pallas import tpu as pltpu
from jax.sharding import Mesh, PartitionSpec as P

time_step = 0.25
viscosity = 0.1
resistivity = 0.08
conduction = 0.12
buoyancy = 0.5
gradient = 0.5

AXES = ("panel", "z", "core", "y", "xh")
SIZES = dict(zip(AXES, (2, 8, 2, 4, 2)))
LAT = ("z", "core")
LON = ("y", "xh")

FIELDS = 14
CT = 24
CP = 576
ROWS = 32
COLS = 640
HALO = 4
SLOTS = 48
NT = 384
LANES = 128
TILES = 128
LANE_TILES = COLS // LANES
LAST = COLS - LANES
VMEM_LIMIT = 24 * 1024 * 1024


def lane_of(shape):
    return lax.broadcasted_iota(jnp.int32, shape, len(shape) - 1)


def row_of(shape):
    return lax.broadcasted_iota(jnp.int32, shape, len(shape) - 2)


def lane_gather(block, index):
    return jnp.take_along_axis(block, index, axis=1, mode="promise_in_bounds")


def add_donors(totals, block_of, index, weight, rb, t):
    for f in range(FIELDS):
        term = weight * lane_gather(block_of(f, rb, t), index)
        totals[f] = term if totals[f] is None else totals[f] + term


def packed_rows(totals):
    rows = [jnp.sum(total, axis=0, keepdims=True) for total in totals]
    rows += [jnp.zeros((1, LANES), jnp.float32)] * (16 - FIELDS)
    packet = jnp.concatenate(rows, axis=0)
    return packet + pltpu.roll(packet, 64, 1)


def build_packet(block_of, index_ref, weight_ref):
    totals = [None] * FIELDS
    for t in range(LANE_TILES):
        for rb in range(CT // 8):
            add_donors(totals, block_of, index_ref[t], weight_ref[rb * LANE_TILES + t], rb, t)
    return packed_rows(totals)


def state_block(state_ref, f, rb, t):
    rows = slice(rb * 8, rb * 8 + 8)
    if t < LANE_TILES - 1:
        return state_ref[f, rows, t * LANES : (t + 1) * LANES]
    half = state_ref[f, rows, LAST:CP]
    return jnp.concatenate([half, jnp.zeros((8, LANES - 64), jnp.float32)], axis=1)


def place_of(aux_ref):
    return aux_ref[7, 0].astype(jnp.int32), aux_ref[7, LANES].astype(jnp.int32)


def open_kernel(
    flags_ref, state_hbm, cell_hbm, frac_hbm, ns_source_hbm, we_source_hbm, ns_turn_hbm, we_turn_hbm,
    state_ref, aux_ref, packet_ref, inner_ref, cross_ref, index_ref, weight_ref,
    cell_ref, frac_ref, ns_source_ref, we_source_ref, ns_turn_ref, we_turn_ref, semaphores,
):
    sources = (cell_hbm, frac_hbm, ns_source_hbm, we_source_hbm, ns_turn_hbm, we_turn_hbm, state_hbm)
    targets = (cell_ref, frac_ref, ns_source_ref, we_source_ref, ns_turn_ref, we_turn_ref, state_ref)
    copies = [pltpu.make_async_copy(sources[i], targets[i], semaphores.at[i]) for i in range(len(sources))]
    for copy in copies:
        copy.start()
    for copy in copies[:-1]:
        copy.wait()
    panel = flags_ref[2, 0]
    far_south = flags_ref[0, 0] >= NT // CT - 2
    far_east = flags_ref[1, 0] == 7
    aux_ref[...] = jnp.zeros((8, COLS), jnp.float32)
    for i, (table, far) in enumerate(
        ((ns_source_ref, far_south), (ns_turn_ref, far_south), (we_source_ref, far_east), (we_turn_ref, far_east))
    ):
        both = table[panel].astype(jnp.float32)
        aux_ref[i : i + 1, 0 : both.shape[1]] = jnp.where(far, both[1:2, :], both[0:1, :])
    aux_ref[7:8, 0:LANES] = flags_ref[0:1, :].astype(jnp.float32)
    aux_ref[7:8, LANES : 2 * LANES] = flags_ref[1:2, :].astype(jnp.float32)
    shape = (8, LANES)
    lane = lane_of(shape)
    row = row_of(shape)
    copies[-1].wait()
    first_core = (flags_ref[0, 0] & 1) == 0
    for c in range(7):
        for t in range(LANE_TILES):
            cols = slice(t * LANES, (t + 1) * LANES)
            top = [state_block(state_ref, 2 * c + k, 0, t) for k in range(2)]
            end = [state_block(state_ref, 2 * c + k, CT // 8 - 1, t) for k in range(2)]
            north = jnp.where(row < HALO, top[0], pltpu.roll(top[1], HALO, 0))
            south = jnp.where(row < HALO, pltpu.roll(end[0], HALO, 0), end[1])
            inner_ref[c, :, cols] = jnp.where(first_core, south, north)
            cross_ref[c, :, cols] = jnp.where(first_core, north, south)

    def doubled(line):
        line = jnp.concatenate([line, jnp.zeros((1, LANES - SLOTS), jnp.float32)], axis=1)
        line = jnp.broadcast_to(line, shape)
        return jnp.where(lane < 64, line, pltpu.roll(line, 64, 1))

    cell = doubled(cell_ref[...].astype(jnp.float32))
    frac_u = doubled(frac_ref[0:1, :])
    frac_v = doubled(frac_ref[1:2, :])
    lat_off = jnp.floor((cell + 0.5) * (1.0 / (CP - 1)))
    lon_off = cell - lat_off * (CP - 1)
    lat_off = lat_off.astype(jnp.int32)
    second = lane >= 64
    column = lon_off.astype(jnp.int32) + second.astype(jnp.int32)
    used = (lane & 63) < SLOTS
    along = jnp.where(second, frac_v, 1.0 - frac_v)
    for t in range(LANE_TILES):
        local = column - t * LANES
        inside = used & (local >= 0) & (local < LANES)
        index_ref[t] = jnp.where(inside, local, 0)
        for rb in range(CT // 8):
            here = row + rb * 8
            down = jnp.where(here == lat_off, 1.0 - frac_u, jnp.where(here == lat_off + 1, frac_u, 0.0))
            weight_ref[rb * LANE_TILES + t] = jnp.where(inside, down * along, 0.0)
    packet_ref[...] = build_packet(functools.partial(state_block, state_ref), index_ref, weight_ref)

    inner_ref[7] = aux_ref[...]
    cross_ref[7] = aux_ref[...]


def ordered(flag, inner, cross):
    first = (flag & 1) == 0
    return jnp.where(first, inner, cross), jnp.where(first, cross, inner)


def outer_rows(from_south, from_north, k, row):
    if k == 0:
        return jnp.where(row < HALO, from_south, pltpu.roll(from_north, HALO, 0))
    return jnp.where(row < HALO, pltpu.roll(from_south, HALO, 0), from_north)


def column_list(aux_ref, lat_inner_ref, lat_cross_ref):
    lane = lane_of((8, LANES))
    block = aux_ref[:, 0:LANES]
    south, north = ordered(place_of(aux_ref)[0], lat_inner_ref[7, :, 0:LANES], lat_cross_ref[7, :, 0:LANES])
    block = jnp.where((lane >= CT) & (lane < CT + HALO), pltpu.roll(south, CT, 1), block)
    return jnp.where((lane >= ROWS - HALO) & (lane < ROWS), pltpu.roll(north, 8, 1), block)


def donor_places(source):
    whole = jnp.floor((source + 0.5) * (1.0 / SLOTS))
    tile = whole.astype(jnp.int32)
    return (source - whole * SLOTS).astype(jnp.int32) + 64 * (tile & 1), tile // 2


def side_kernel(aux_ref, state_ref, lat_inner_ref, lat_cross_ref, inner_ref, cross_ref, column_ref):
    shape = (8, LANES)
    source = jnp.broadcast_to(column_list(aux_ref, lat_inner_ref, lat_cross_ref)[2:3, :], shape)
    column_ref[0:8, :], column_ref[8:16, :] = donor_places(source)
    lat, lon = place_of(aux_ref)
    lane = lane_of(shape)
    row = row_of(shape)
    for rb in range(ROWS // 8):
        west = jnp.zeros(shape, jnp.float32)
        east = jnp.zeros(shape, jnp.float32)
        for f in range(FIELDS):
            c, k = f // 2, f % 2
            if rb < CT // 8:
                first = state_block(state_ref, f, rb, 0)
                last = state_block(state_ref, f, rb, LANE_TILES - 1)
            else:
                first = outer_rows(*ordered(lat, lat_inner_ref[c, :, 0:LANES], lat_cross_ref[c, :, 0:LANES]), k, row)
                last = outer_rows(*ordered(lat, lat_inner_ref[c, :, LAST:COLS], lat_cross_ref[c, :, LAST:COLS]), k, row)
            here = (lane >= 8 * f) & (lane < 8 * f + HALO)
            west = jnp.where(here, pltpu.roll(first, 8 * f, 1) if f else first, west)
            east = jnp.where(here, pltpu.roll(last, (8 * f - 60) % LANES, 1), east)
        if rb == 0:
            here = (lane >= 112) & (lane < 112 + HALO)
            west = jnp.where(here, pltpu.roll(aux_ref[:, 0:LANES], 112, 1), west)
            east = jnp.where(here, pltpu.roll(aux_ref[:, LAST:COLS], 112 - 60, 1), east)
        inner, cross = ordered(lon, east, west)
        inner_ref[rb * 8 : rb * 8 + 8, :] = inner
        cross_ref[rb * 8 : rb * 8 + 8, :] = cross


def with_columns(block, from_east, from_west, f, lane):
    block = jnp.where((lane >= 64) & (lane < 64 + HALO), pltpu.roll(from_east, (64 - 8 * f) % LANES, 1), block)
    return jnp.where(lane >= LANES - HALO, pltpu.roll(from_west, (124 - 8 * f) % LANES, 1), block)


def frame_kernel(
    aux_ref, state_ref, lat_inner_ref, lat_cross_ref, lon_inner_ref, lon_cross_ref,
    full_ref, slot_ref, tile_ref, cos_ref, sin_ref, metric_ref,
):
    shape = (8, LANES)
    lat, lon = place_of(aux_ref)
    lane = lane_of(shape)
    row = row_of(shape)
    for rb in range(ROWS // 8):
        rows = slice(rb * 8, rb * 8 + 8)
        east, west = ordered(lon, lon_inner_ref[rows, :], lon_cross_ref[rows, :])
        for f in range(FIELDS):
            c, k = f // 2, f % 2
            for t in range(LANE_TILES):
                cols = slice(t * LANES, (t + 1) * LANES)
                if rb < CT // 8:
                    block = state_block(state_ref, f, rb, t)
                else:
                    south, north = ordered(lat, lat_inner_ref[c, :, cols], lat_cross_ref[c, :, cols])
                    block = outer_rows(south, north, k, row)
                if t == LANE_TILES - 1:
                    block = with_columns(block, east, west, f, lane)
                full_ref[f, rows, cols] = block
    for t in range(LANE_TILES + 1):
        if t < LANE_TILES:
            block = aux_ref[:, t * LANES : (t + 1) * LANES]
            if t == LANE_TILES - 1:
                east, west = ordered(lon, lon_inner_ref[0:8, :], lon_cross_ref[0:8, :])
                block = jnp.where((lane >= 64) & (lane < 64 + HALO), pltpu.roll(east, (64 - 112) % LANES, 1), block)
                block = jnp.where(lane >= LANES - HALO, pltpu.roll(west, 124 - 112, 1), block)
            source = jnp.broadcast_to(block[0:1, :], shape)
            angle = jnp.broadcast_to(block[1:2, :], shape)
        else:
            block = column_list(aux_ref, lat_inner_ref, lat_cross_ref)
            source = jnp.broadcast_to(block[2:3, :], shape)
            angle = jnp.broadcast_to(block[3:4, :], shape)
        slot_ref[t], tile_ref[t] = donor_places(source)
        cos_ref[t] = jnp.cos(angle)
        sin_ref[t] = jnp.sin(angle)
    line = row_of((ROWS, LANES))
    line = jnp.where(line >= ROWS - HALO, line - ROWS, line) + lat * CT
    theta = math.pi / 4 + (line.astype(jnp.float32) + 0.5) * ((math.pi / 2) / NT)
    metric_ref[...] = 1.0 / jnp.sin(theta)


def pick_kernel(aux_ref, donor_ref, slot_ref, tile_ref, other_ref, out_ref):
    mine = 4 * (place_of(aux_ref)[0] & 1)
    count = LANE_TILES + 1
    tables = [(slot_ref[t], tile_ref[t]) for t in range(count)] + [(other_ref[0:8, :], other_ref[8:16, :])]
    for t, (slots, pairs) in enumerate(tables):
        pairs = pairs - mine
        low = jnp.zeros((8, LANES), jnp.float32)
        high = jnp.zeros((8, LANES), jnp.float32)
        for v in range(TILES // 4):
            here = pairs == v % 8 * 8 + v // 8
            low = jnp.where(here, lane_gather(donor_ref[v, 0:8, :], slots), low)
            high = jnp.where(here, lane_gather(donor_ref[v, 8:16, :], slots), high)
        out_ref[t, 0:8, :] = low
        out_ref[t, 8:16, :] = high


def turned_ghosts(share_ref, other_ref, cos_ref, sin_ref):
    shape = (8, LANES)
    row = row_of(shape)
    count = LANE_TILES + 1
    low, high = [], []
    for t in range(count):
        theirs = t if t < LANE_TILES else count
        for out, rows in ((low, slice(0, 8)), (high, slice(8, 16))):
            out.append(share_ref[t, rows, :] + other_ref[theirs, rows, :])
    ghosts = []
    for t in range(count):
        cosine, sine = cos_ref[t], sin_ref[t]
        first = (row == 2) | (row == 3)
        other = (row == 4) | (row == 5)
        mate = jnp.where(first, pltpu.roll(low[t], 6, 0), pltpu.roll(low[t], 2, 0))
        turn = jnp.where(first, -sine, sine)
        a = jnp.where(first | other, cosine * low[t] + turn * mate, low[t])
        first = row < 2
        mate = jnp.where(first, pltpu.roll(high[t], 6, 0), pltpu.roll(high[t], 2, 0))
        turn = jnp.where(first, -sine, sine)
        b = jnp.where(row < 4, cosine * high[t] + turn * mate, high[t])
        ghosts.append((a, b))
    return ghosts


def keep_ghosts(lon, ghosts, line_ref, column_ref):
    for t in range(LANE_TILES):
        cols = slice(t * LANES, (t + 1) * LANES)
        line_ref[0:8, cols], line_ref[8:16, cols] = ghosts[t]

    def put_column():
        shape = (ROWS, LANES)
        diagonal = lane_of(shape) == row_of(shape)
        for f in range(FIELDS):
            values = jnp.broadcast_to(ghosts[LANE_TILES][f // 8][f % 8 : f % 8 + 1, :], shape)
            column = jnp.sum(jnp.where(diagonal, values, 0.0), axis=1, keepdims=True)
            column_ref[f] = jnp.broadcast_to(column, shape)

    pl.when((lon == 0) | (lon == 7))(put_column)


def tendency(work_ref, metric_ref, rb, k, emit, tile=None, ghosts=None):
    low = rb * 8
    rows = slice(low, low + 8)
    whole = tile is None
    cols = slice(0, COLS) if whole else slice(tile * LANES, (tile + 1) * LANES)
    shape = (8, cols.stop - cols.start)
    row = row_of(shape)
    lane = lane_of(shape)
    metric = metric_ref[rows, :]
    if whole:
        metric = jnp.concatenate([metric] * LANE_TILES, axis=1)
    square = metric * metric
    centre_weight = 4.0 + 2.0 * square
    radial = 0.5 if k == 0 else -0.5

    def value(c):
        return work_ref[2 * c + k, rows, cols]

    def beside(f, step):
        start = (tile + step) % LANE_TILES * LANES
        return work_ref[f, rows, start : start + LANES]

    def coefficients(c):
        return radial * value(c), 0.5 * value(c + 1), (0.5 * metric) * value(c + 2)

    flow_by = coefficients(0)
    field_by = coefficients(3)

    def parts(c):
        f = 2 * c + k
        centre = value(c)
        across = work_ref[2 * c + 1 - k, rows, cols]
        before = work_ref[f, (low - 1) % ROWS : (low - 1) % ROWS + 1, cols]
        after = work_ref[f, (low + 8) % ROWS : (low + 8) % ROWS + 1, cols]
        if ghosts is not None:
            (lat, lon), line_ref, column_ref = ghosts
            if rb == 0:
                before = jnp.where(lat == 0, line_ref[f : f + 1, cols], before)
            if rb == CT // 8 - 1:
                after = jnp.where(lat == NT // CT - 1, line_ref[f : f + 1, cols], after)
        north = jnp.where(row == 0, jnp.broadcast_to(before, shape), pltpu.roll(centre, 1, 0))
        south = jnp.where(row == 7, jnp.broadcast_to(after, shape), pltpu.roll(centre, 7, 0))
        west = pltpu.roll(centre, 1, 1)
        east = pltpu.roll(centre, shape[1] - 1, 1)
        if tile == 0:
            west = jnp.where(lane == 0, jnp.where(lon == 0, column_ref[f, rows, :], pltpu.roll(beside(f, -1), 1, 1)), west)
            east = jnp.where(lane == LANES - 1, pltpu.roll(beside(f, 1), LANES - 1, 1), east)
        elif tile is not None:
            west = jnp.where(lane == 0, pltpu.roll(beside(f, -1), 1, 1), west)
            east = jnp.where(lane == LANES - 1, pltpu.roll(beside(f, 1), LANES - 1, 1), east)
            east = jnp.where((lane == CP - LAST - 1) & (lon == 7), column_ref[f, rows, :], east)
        grad_t = south - north
        grad_p = east - west
        laplace = across + (south + north) + square * (east + west) - centre_weight * centre
        return across, grad_t, grad_p, laplace

    def along(by, p):
        return by[0] * p[0] + by[1] * p[1] + by[2] * p[2]

    for c in range(3):
        p = parts(c)
        u_flow, u_field, u_laplace = along(flow_by, p), along(field_by, p), p[3]
        p = parts(c + 3)
        velocity = along(field_by, p) - u_flow + viscosity * u_laplace
        if c == 0:
            velocity = velocity + buoyancy * value(6)
        emit(c, velocity)
        emit(c + 3, u_field - along(flow_by, p) + resistivity * p[3])
    p = parts(6)
    emit(6, conduction * p[3] - along(flow_by, p) + gradient * value(0))


def inner_kernel(factor, metric_ref, full_ref, now_ref, next_ref):
    for rb in range(ROWS // 8):
        rows = slice(rb * 8, rb * 8 + 8)
        for k in range(2):

            def emit(c, value):
                next_ref[2 * c + k, rows, :] = full_ref[2 * c + k, rows, :] + factor * value

            tendency(now_ref, metric_ref, rb, k, emit)


def first_inner_kernel(metric_ref, full_ref, next_ref):
    inner_kernel(time_step / 2, metric_ref, full_ref, full_ref, next_ref)


def put_rim(place, inner_ref, row_ref, column_ref, now_ref):
    lat, lon = place
    now_ref[...] = inner_ref[...]

    def put_row(rb):
        now_ref[:, rb * 8 : rb * 8 + 8, :] = row_ref[...]

    def put_column(tile):
        now_ref[:, :, tile * LANES : (tile + 1) * LANES] = column_ref[...]

    pl.when(lat == 0)(lambda: put_row(0))
    pl.when(lat == NT // CT - 1)(lambda: put_row(CT // 8 - 1))
    pl.when(lon == 0)(lambda: put_column(0))
    pl.when(lon == 7)(lambda: put_column(LANE_TILES - 1))


def next_inner_kernel(factor, aux_ref, metric_ref, full_ref, inner_ref, row_ref, column_ref, now_ref, next_ref):
    put_rim(place_of(aux_ref), inner_ref, row_ref, column_ref, now_ref)
    inner_kernel(factor, metric_ref, full_ref, now_ref, next_ref)


def on_rim(place, rb, t):
    lat, lon = place
    in_row = {0: lat == 0, CT // 8 - 1: lat == NT // CT - 1}.get(rb, False)
    in_column = {0: lon == 0, LANE_TILES - 1: lon == 7}.get(t, False)
    return in_row, in_column


def donor_kernel(aux_ref, inner_ref, index_ref, weight_ref, total_ref):
    place = place_of(aux_ref)
    totals = [None] * FIELDS

    def block_of(f, rb, t):
        return inner_ref[f, rb * 8 : rb * 8 + 8, t * LANES : (t + 1) * LANES]

    for t in range(LANE_TILES):
        for rb in range(CT // 8):
            weight = weight_ref[rb * LANE_TILES + t]
            for here in on_rim(place, rb, t):
                if here is not False:
                    weight = jnp.where(here, 0.0, weight)
            add_donors(totals, block_of, index_ref[t], weight, rb, t)
    for f in range(FIELDS):
        total_ref[f] = totals[f]


def redo_rim(place, now_ref, metric_ref, line_ref, column_ref, blocks, store):
    lat, lon = place

    def redo(rbs, tile):
        cols = slice(0, COLS) if tile is None else slice(tile * LANES, (tile + 1) * LANES)
        for rb in rbs:
            for k in range(2):

                def emit(c, value):
                    store(2 * c + k, slice(rb * 8, rb * 8 + 8), cols, value)

                tendency(now_ref, metric_ref, rb, k, emit, tile, (place, line_ref, column_ref))

    pl.when(lat == 0)(lambda: redo([0], None))
    pl.when(lat == NT // CT - 1)(lambda: redo([CT // 8 - 1], None))
    pl.when(lon == 0)(lambda: redo(range(blocks), 0))
    pl.when(lon == 7)(lambda: redo(range(blocks), LANE_TILES - 1))


def rim_kernel(
    factor, aux_ref, share_ref, other_ref, cos_ref, sin_ref, metric_ref, index_ref, weight_ref, total_ref, full_ref, now_ref,
    row_ref, side_ref, packet_ref, line_ref, column_ref, sum_ref,
):
    place = place_of(aux_ref)
    lat, lon = place
    keep_ghosts(lon, turned_ghosts(share_ref, other_ref, cos_ref, sin_ref), line_ref, column_ref)
    sum_ref[...] = total_ref[...]

    def store(f, rows, cols, value):
        value = full_ref[f, rows, cols] + factor * value
        if cols.stop - cols.start == COLS:
            row_ref[f] = value
        else:
            side_ref[f, rows, :] = value

    redo_rim(place, now_ref, metric_ref, line_ref, column_ref, ROWS // 8, store)

    def add(blocks, block_of, skip):
        totals = [sum_ref[f] for f in range(FIELDS)]
        for rb, t in blocks:
            weight = weight_ref[rb * LANE_TILES + t]
            if skip and on_rim(place, rb, t)[1] is not False:
                weight = jnp.where(on_rim(place, rb, t)[1], 0.0, weight)
            add_donors(totals, block_of, index_ref[t], weight, rb, t)
        for f in range(FIELDS):
            sum_ref[f] = totals[f]

    def add_row(rb):
        blocks = [(rb, t) for t in range(LANE_TILES)]
        add(blocks, lambda f, rb, t: row_ref[f, :, t * LANES : (t + 1) * LANES], True)

    def add_side(t):
        blocks = [(rb, t) for rb in range(CT // 8)]
        add(blocks, lambda f, rb, t: side_ref[f, rb * 8 : rb * 8 + 8, :], False)

    pl.when(lat == 0)(lambda: add_row(0))
    pl.when(lat == NT // CT - 1)(lambda: add_row(CT // 8 - 1))
    pl.when(lon == 0)(lambda: add_side(0))
    pl.when(lon == 7)(lambda: add_side(LANE_TILES - 1))
    packet_ref[...] = packed_rows([sum_ref[f] for f in range(FIELDS)])


def last_inner_kernel(
    aux_ref, metric_ref, full_ref, second_ref, third_ref, inner_ref, row_ref, column_ref, fourth_ref, base_ref, out_ref
):
    put_rim(place_of(aux_ref), inner_ref, row_ref, column_ref, fourth_ref)
    for rb in range(CT // 8):
        rows = slice(rb * 8, rb * 8 + 8)
        for k in range(2):

            def emit(c, value):
                f = 2 * c + k
                base = second_ref[f, rows, :] + 2.0 * third_ref[f, rows, :] + fourth_ref[f, rows, :] - full_ref[f, rows, :]
                base = (1.0 / 3.0) * base
                base_ref[f, rows, :] = base
                out_ref[f, rows, :] = base + (time_step / 6) * value

            tendency(fourth_ref, metric_ref, rb, k, emit)


def last_rim_kernel(
    aux_ref, share_ref, other_ref, cos_ref, sin_ref, metric_ref, base_ref, inner_ref, now_ref,
    out_ref, line_ref, column_ref,
):
    place = place_of(aux_ref)
    keep_ghosts(place[1], turned_ghosts(share_ref, other_ref, cos_ref, sin_ref), line_ref, column_ref)
    for f in range(FIELDS):
        out_ref[f] = inner_ref[f, :, 0:CP]

    def store(f, rows, cols, value):
        cols = slice(cols.start, min(cols.stop, CP))
        out = base_ref[f, rows, cols] + (time_step / 6) * value[:, : cols.stop - cols.start]
        out_ref[f, rows, cols] = out

    redo_rim(place, now_ref, metric_ref, line_ref, column_ref, CT // 8, store)


def call(kernel, ins, outs, scratch=(), cost=0, left=()):
    vmem = pl.BlockSpec(memory_space=pltpu.VMEM)
    hbm = pl.BlockSpec(memory_space=pltpu.HBM)
    shapes = tuple(jax.ShapeDtypeStruct(s, d) for s, d in outs)
    ins = [pltpu.with_memory_space_constraint(a, pltpu.HBM) if i in left else a for i, a in enumerate(ins)]
    return pl.pallas_call(
        kernel,
        out_shape=shapes,
        in_specs=[hbm if i in left else vmem for i in range(len(ins))],
        out_specs=(vmem,) * len(outs),
        scratch_shapes=list(scratch),
        compiler_params=pltpu.CompilerParams(vmem_limit_bytes=VMEM_LIMIT),
        cost_estimate=pl.CostEstimate(flops=cost * 1000, bytes_accessed=cost, transcendentals=0) if cost else None,
    )(*ins)


def coordinates(axes):
    points = [()]
    for a in axes:
        points = [q + (i,) for q in points for i in range(SIZES[a])]
    return points


def permute(value, axes, move):
    points = coordinates(axes)
    place = {q: i for i, q in enumerate(points)}
    pairs = []
    for q in points:
        to = move(q)
        if to is not None:
            pairs.append((place[q], place[to]))
    return lax.ppermute(value, axes if len(axes) > 1 else axes[0], pairs)


def within(value, axes):
    return permute(value, axes, lambda q: (q[0], 1 - q[1]))


def between(value, axes):
    count = SIZES[axes[0]]
    return permute(value, axes, lambda q: ((q[0] + 1) % count, 0) if q[1] == 1 else ((q[0] - 1) % count, 1))


def swap_packets(packet):
    same = permute(packet, ("panel", "xh"), lambda q: (1 - q[0], q[1]))
    other = permute(packet, ("panel", "xh"), lambda q: (1 - q[0], 1 - q[1]))
    second = lane_of(packet.shape) >= 64
    return jnp.where(second == (lax.axis_index("xh") == 1), same, other)


def spread_packets(pair):
    count = SIZES["z"] * SIZES["y"]
    return lax.all_to_all(jnp.broadcast_to(pair[None], (count,) + pair.shape), ("y", "z"), 0, 0)


def other_core(value):
    return permute(value, ("core",), lambda q: (1 - q[0],))


def on_device(state, pack_cell, pack_frac, ns_source, we_source, ns_turn, we_turn):
    f32 = jnp.float32
    tile = state.reshape(FIELDS, CT, CP)
    lat = lax.axis_index(LAT)
    lon = lax.axis_index(LON)
    panel = lax.axis_index("panel")
    flags = jnp.broadcast_to(jnp.stack([lat, lon, panel] + [panel] * 5).astype(jnp.int32)[:, None], (8, LANES))
    raw = [pack_cell.reshape(1, SLOTS), pack_frac.reshape(2, SLOTS), ns_source, we_source, ns_turn, we_turn]
    vreg = (8, LANES)
    packed = ((16, LANES), f32)
    whole = ((FIELDS, ROWS, COLS), f32)
    message = ((8, 8, COLS), f32)
    side = ((ROWS, LANES), f32)
    tile, aux, packet, lat_inner, lat_cross, index, weight = call(
        open_kernel,
        [flags, tile] + raw,
        [
            ((FIELDS, CT, CP), f32),
            ((8, COLS), f32),
            packed,
            message,
            message,
            ((LANE_TILES,) + vreg, jnp.int32),
            ((3 * LANE_TILES,) + vreg, f32),
        ],
        scratch=[pltpu.VMEM(a.shape, a.dtype) for a in raw] + [pltpu.SemaphoreType.DMA((len(raw) + 1,))],
        left=range(1, 8),
    )
    lat_inner = within(lat_inner, LAT)
    lat_cross = between(lat_cross, LAT)
    lon_inner, lon_cross, column = call(
        side_kernel, [aux, tile, lat_inner, lat_cross], [side, side, ((16, LANES), jnp.int32)], cost=8_000_000
    )
    column = other_core(column)
    pair = swap_packets(packet)
    lon_inner = within(lon_inner, LON)
    lon_cross = between(lon_cross, LON)
    donors = spread_packets(pair)
    donors, lon_inner, lon_cross = lax.optimization_barrier((donors, lon_inner, lon_cross))
    points = (LANE_TILES + 1,) + vreg
    full, slot, where, cosine, sine, metric = call(
        frame_kernel,
        [aux, tile, lat_inner, lat_cross, lon_inner, lon_cross],
        [whole, (points, jnp.int32), (points, jnp.int32), (points, f32), (points, f32), ((ROWS, LANES), f32)],
    )
    lists = [slot, where, column]
    kept = [pltpu.VMEM((16, COLS), f32), pltpu.VMEM((FIELDS, ROWS, LANES), f32)]

    def ghost_tables(donors):
        (share,) = call(pick_kernel, [aux, donors] + lists, [((LANE_TILES + 2, 16, LANES), f32)])
        return [aux, share, other_core(share), cosine, sine, metric]

    row, side = ((FIELDS, 8, COLS), f32), ((FIELDS, ROWS, LANES), f32)
    totals = ((FIELDS,) + vreg, f32)
    states = [full]
    for factor in (time_step / 2, time_step / 2, time_step):
        if len(states) == 1:
            (inner,) = call(first_inner_kernel, [metric, full], [whole], cost=2_000_000)
        else:
            pair = swap_packets(packet)
            now, inner = call(
                functools.partial(next_inner_kernel, factor), [aux, metric, full, inner] + rim, [whole, whole], cost=2_000_000
            )
            states[-1] = now
            pair, inner = lax.optimization_barrier((pair, inner))
            donors = spread_packets(pair)
        tables = ghost_tables(donors)
        (sums,) = call(donor_kernel, [aux, inner, index, weight], [totals], cost=500_000)
        *rim, packet = call(
            functools.partial(rim_kernel, factor),
            tables + [index, weight, sums, full, states[-1]],
            [row, side, packed],
            scratch=kept + [pltpu.VMEM(*totals)],
        )
        states.append(None)
    pair = swap_packets(packet)
    inner_shape = ((FIELDS, CT, COLS), f32)
    states[-1], base, inner = call(
        last_inner_kernel, [aux, metric] + states[:-1] + [inner] + rim, [whole, inner_shape, inner_shape], cost=2_000_000
    )
    pair, inner = lax.optimization_barrier((pair, inner))
    (result,) = call(
        last_rim_kernel,
        ghost_tables(spread_packets(pair)) + [base, inner, states[-1]],
        [((FIELDS, CT, CP), f32)],
        scratch=kept,
    )
    return result.reshape(state.shape)


def solution(mesh):
    fine = Mesh(mesh.devices.reshape(tuple(SIZES[a] for a in AXES)), AXES)
    return jax.shard_map(
        on_device,
        mesh=fine,
        in_specs=(
            P("panel", None, None, LAT, LON),
            P("panel", LAT, LON, None),
            P("panel", None, LAT, LON, None),
            P(None, None, LON),
            P(None, None, LAT),
            P(None, None, LON),
            P(None, None, LAT),
        ),
        out_specs=P("panel", None, None, LAT, LON),
        check_vma=False,
    )
```

```python
import functools
import math

import jax
import jax.numpy as jnp
from jax import lax
from jax.experimental import pallas as pl
from jax.experimental.pallas import tpu as pltpu
from jax.sharding import Mesh, PartitionSpec as P

time_step = 0.25
viscosity = 0.1
resistivity = 0.08
conduction = 0.12
buoyancy = 0.5
gradient = 0.5

AXES = ("panel", "z", "core", "y", "xh")
SIZES = dict(zip(AXES, (2, 8, 2, 4, 2)))
LAT = ("z", "core")
LON = ("y", "xh")

FIELDS = 14
CT = 24
CP = 576
ROWS = 32
COLS = 640
HALO = 4
SLOTS = 48
NT = 384
LANES = 128
TILES = 128
LANE_TILES = COLS // LANES
LAST = COLS - LANES
VMEM_LIMIT = 24 * 1024 * 1024


def lane_of(shape):
    return lax.broadcasted_iota(jnp.int32, shape, len(shape) - 1)


def row_of(shape):
    return lax.broadcasted_iota(jnp.int32, shape, len(shape) - 2)


def lane_gather(block, index):
    return jnp.take_along_axis(block, index, axis=1, mode="promise_in_bounds")


def add_donors(totals, block_of, index, weight, rb, t):
    for f in range(FIELDS):
        term = weight * lane_gather(block_of(f, rb, t), index)
        totals[f] = term if totals[f] is None else totals[f] + term


def packed_rows(totals):
    rows = [jnp.sum(total, axis=0, keepdims=True) for total in totals]
    rows += [jnp.zeros((1, LANES), jnp.float32)] * (16 - FIELDS)
    packet = jnp.concatenate(rows, axis=0)
    return packet + pltpu.roll(packet, 64, 1)


def build_packet(block_of, index_ref, weight_ref):
    totals = [None] * FIELDS
    for t in range(LANE_TILES):
        for rb in range(CT // 8):
            add_donors(totals, block_of, index_ref[t], weight_ref[rb * LANE_TILES + t], rb, t)
    return packed_rows(totals)


def state_block(state_ref, f, rb, t):
    rows = slice(rb * 8, rb * 8 + 8)
    if t < LANE_TILES - 1:
        return state_ref[f, rows, t * LANES : (t + 1) * LANES]
    half = state_ref[f, rows, LAST:CP]
    return jnp.concatenate([half, jnp.zeros((8, LANES - 64), jnp.float32)], axis=1)


def place_of(aux_ref):
    return aux_ref[7, 0].astype(jnp.int32), aux_ref[7, LANES].astype(jnp.int32)


def open_kernel(
    flags_ref, state_hbm, cell_hbm, frac_hbm, ns_source_hbm, we_source_hbm, ns_turn_hbm, we_turn_hbm,
    state_ref, aux_ref, packet_ref, inner_ref, cross_ref, index_ref, weight_ref,
    cell_ref, frac_ref, ns_source_ref, we_source_ref, ns_turn_ref, we_turn_ref, semaphores,
):
    sources = (cell_hbm, frac_hbm, ns_source_hbm, we_source_hbm, ns_turn_hbm, we_turn_hbm, state_hbm)
    targets = (cell_ref, frac_ref, ns_source_ref, we_source_ref, ns_turn_ref, we_turn_ref, state_ref)
    copies = [pltpu.make_async_copy(sources[i], targets[i], semaphores.at[i]) for i in range(len(sources))]
    for copy in copies:
        copy.start()
    for copy in copies[:-1]:
        copy.wait()
    panel = flags_ref[2, 0]
    far_south = flags_ref[0, 0] >= NT // CT - 2
    far_east = flags_ref[1, 0] == 7
    aux_ref[...] = jnp.zeros((8, COLS), jnp.float32)
    for i, (table, far) in enumerate(
        ((ns_source_ref, far_south), (ns_turn_ref, far_south), (we_source_ref, far_east), (we_turn_ref, far_east))
    ):
        both = table[panel].astype(jnp.float32)
        aux_ref[i : i + 1, 0 : both.shape[1]] = jnp.where(far, both[1:2, :], both[0:1, :])
    aux_ref[7:8, 0:LANES] = flags_ref[0:1, :].astype(jnp.float32)
    aux_ref[7:8, LANES : 2 * LANES] = flags_ref[1:2, :].astype(jnp.float32)
    shape = (8, LANES)
    lane = lane_of(shape)
    row = row_of(shape)
    copies[-1].wait()
    for rb in range(CT // 8):
        west = jnp.zeros(shape, jnp.float32)
        east = jnp.zeros(shape, jnp.float32)
        for f in range(FIELDS):
            first = state_block(state_ref, f, rb, 0)
            last = state_block(state_ref, f, rb, LANE_TILES - 1)
            here = (lane >= 8 * f) & (lane < 8 * f + HALO)
            west = jnp.where(here, pltpu.roll(first, 8 * f, 1) if f else first, west)
            east = jnp.where(here, pltpu.roll(last, (8 * f - 60) % LANES, 1), east)
        if rb == 0:
            here = (lane >= 112) & (lane < 112 + HALO)
            west = jnp.where(here, pltpu.roll(aux_ref[:, 0:LANES], 112, 1), west)
            east = jnp.where(here, pltpu.roll(aux_ref[:, LAST:COLS], 112 - 60, 1), east)
        rows = slice(rb * 8, rb * 8 + 8)
        inner_ref[rows, :], cross_ref[rows, :] = ordered(flags_ref[1, 0], east, west)

    def doubled(line):
        line = jnp.concatenate([line, jnp.zeros((1, LANES - SLOTS), jnp.float32)], axis=1)
        line = jnp.broadcast_to(line, shape)
        return jnp.where(lane < 64, line, pltpu.roll(line, 64, 1))

    cell = doubled(cell_ref[...].astype(jnp.float32))
    frac_u = doubled(frac_ref[0:1, :])
    frac_v = doubled(frac_ref[1:2, :])
    lat_off = jnp.floor((cell + 0.5) * (1.0 / (CP - 1)))
    lon_off = cell - lat_off * (CP - 1)
    lat_off = lat_off.astype(jnp.int32)
    second = lane >= 64
    column = lon_off.astype(jnp.int32) + second.astype(jnp.int32)
    used = (lane & 63) < SLOTS
    along = jnp.where(second, frac_v, 1.0 - frac_v)
    for t in range(LANE_TILES):
        local = column - t * LANES
        inside = used & (local >= 0) & (local < LANES)
        index_ref[t] = jnp.where(inside, local, 0)
        for rb in range(CT // 8):
            here = row + rb * 8
            down = jnp.where(here == lat_off, 1.0 - frac_u, jnp.where(here == lat_off + 1, frac_u, 0.0))
            weight_ref[rb * LANE_TILES + t] = jnp.where(inside, down * along, 0.0)
    packet_ref[...] = build_packet(functools.partial(state_block, state_ref), index_ref, weight_ref)


def ordered(flag, inner, cross):
    first = (flag & 1) == 0
    return jnp.where(first, inner, cross), jnp.where(first, cross, inner)


def outer_rows(from_south, from_north, k, row):
    if k == 0:
        return jnp.where(row < HALO, from_south, pltpu.roll(from_north, HALO, 0))
    return jnp.where(row < HALO, pltpu.roll(from_south, HALO, 0), from_north)


def column_list(aux_ref, lat_inner_ref, lat_cross_ref):
    lane = lane_of((8, LANES))
    block = aux_ref[:, 0:LANES]
    south, north = ordered(place_of(aux_ref)[0], lat_inner_ref[7, :, 0:LANES], lat_cross_ref[7, :, 0:LANES])
    block = jnp.where((lane >= CT) & (lane < CT + HALO), pltpu.roll(south, CT, 1), block)
    return jnp.where((lane >= ROWS - HALO) & (lane < ROWS), pltpu.roll(north, 8, 1), block)


def donor_places(source):
    whole = jnp.floor((source + 0.5) * (1.0 / SLOTS))
    tile = whole.astype(jnp.int32)
    return (source - whole * SLOTS).astype(jnp.int32) + 64 * (tile & 1), tile // 2


def lat_kernel(aux_ref, state_ref, lon_inner_ref, lon_cross_ref, inner_ref, cross_ref):
    shape = (8, LANES)
    lane = lane_of(shape)
    row = row_of(shape)
    lat, lon = place_of(aux_ref)
    first_core = (lat & 1) == 0

    def block(f, rb, t):
        value = state_block(state_ref, f, rb, t)
        if t < LANE_TILES - 1:
            return value
        rows = slice(rb * 8, rb * 8 + 8)
        return with_columns(value, *ordered(lon, lon_inner_ref[rows, :], lon_cross_ref[rows, :]), f, lane)

    for c in range(7):
        for t in range(LANE_TILES):
            cols = slice(t * LANES, (t + 1) * LANES)
            top = [block(2 * c + k, 0, t) for k in range(2)]
            end = [block(2 * c + k, CT // 8 - 1, t) for k in range(2)]
            north = jnp.where(row < HALO, top[0], pltpu.roll(top[1], HALO, 0))
            south = jnp.where(row < HALO, pltpu.roll(end[0], HALO, 0), end[1])
            inner_ref[c, :, cols] = jnp.where(first_core, south, north)
            cross_ref[c, :, cols] = jnp.where(first_core, north, south)
    inner_ref[7] = aux_ref[...]
    cross_ref[7] = aux_ref[...]


def with_columns(block, from_east, from_west, f, lane):
    block = jnp.where((lane >= 64) & (lane < 64 + HALO), pltpu.roll(from_east, (64 - 8 * f) % LANES, 1), block)
    return jnp.where(lane >= LANES - HALO, pltpu.roll(from_west, (124 - 8 * f) % LANES, 1), block)


def frame_kernel(
    aux_ref, state_ref, lat_inner_ref, lat_cross_ref, lon_inner_ref, lon_cross_ref,
    full_ref, slot_ref, tile_ref, cos_ref, sin_ref, metric_ref, column_ref,
):
    shape = (8, LANES)
    lat, lon = place_of(aux_ref)
    lane = lane_of(shape)
    row = row_of(shape)
    for rb in range(ROWS // 8):
        rows = slice(rb * 8, rb * 8 + 8)
        for f in range(FIELDS):
            c, k = f // 2, f % 2
            for t in range(LANE_TILES):
                cols = slice(t * LANES, (t + 1) * LANES)
                if rb < CT // 8:
                    block = state_block(state_ref, f, rb, t)
                    if t == LANE_TILES - 1:
                        sides = ordered(lon, lon_inner_ref[rows, :], lon_cross_ref[rows, :])
                        block = with_columns(block, *sides, f, lane)
                else:
                    south, north = ordered(lat, lat_inner_ref[c, :, cols], lat_cross_ref[c, :, cols])
                    block = outer_rows(south, north, k, row)
                full_ref[f, rows, cols] = block
    for t in range(LANE_TILES + 1):
        if t < LANE_TILES:
            block = aux_ref[:, t * LANES : (t + 1) * LANES]
            if t == LANE_TILES - 1:
                east, west = ordered(lon, lon_inner_ref[0:8, :], lon_cross_ref[0:8, :])
                block = jnp.where((lane >= 64) & (lane < 64 + HALO), pltpu.roll(east, (64 - 112) % LANES, 1), block)
                block = jnp.where(lane >= LANES - HALO, pltpu.roll(west, 124 - 112, 1), block)
            source = jnp.broadcast_to(block[0:1, :], shape)
            angle = jnp.broadcast_to(block[1:2, :], shape)
        else:
            block = column_list(aux_ref, lat_inner_ref, lat_cross_ref)
            source = jnp.broadcast_to(block[2:3, :], shape)
            angle = jnp.broadcast_to(block[3:4, :], shape)
        slot_ref[t], tile_ref[t] = donor_places(source)
        if t == LANE_TILES:
            column_ref[0:8, :], column_ref[8:16, :] = donor_places(source)
        cos_ref[t] = jnp.cos(angle)
        sin_ref[t] = jnp.sin(angle)
    line = row_of((ROWS, LANES))
    line = jnp.where(line >= ROWS - HALO, line - ROWS, line) + lat * CT
    theta = math.pi / 4 + (line.astype(jnp.float32) + 0.5) * ((math.pi / 2) / NT)
    metric_ref[...] = 1.0 / jnp.sin(theta)


def pick_kernel(aux_ref, donor_ref, slot_ref, tile_ref, other_ref, out_ref):
    mine = 4 * (place_of(aux_ref)[0] & 1)
    count = LANE_TILES + 1
    tables = [(slot_ref[t], tile_ref[t]) for t in range(count)] + [(other_ref[0:8, :], other_ref[8:16, :])]
    for t, (slots, pairs) in enumerate(tables):
        pairs = pairs - mine
        low = jnp.zeros((8, LANES), jnp.float32)
        high = jnp.zeros((8, LANES), jnp.float32)
        for v in range(TILES // 4):
            here = pairs == v % 8 * 8 + v // 8
            low = jnp.where(here, lane_gather(donor_ref[v, 0:8, :], slots), low)
            high = jnp.where(here, lane_gather(donor_ref[v, 8:16, :], slots), high)
        out_ref[t, 0:8, :] = low
        out_ref[t, 8:16, :] = high


def turned_ghosts(share_ref, other_ref, cos_ref, sin_ref):
    shape = (8, LANES)
    row = row_of(shape)
    count = LANE_TILES + 1
    low, high = [], []
    for t in range(count):
        theirs = t if t < LANE_TILES else count
        for out, rows in ((low, slice(0, 8)), (high, slice(8, 16))):
            out.append(share_ref[t, rows, :] + other_ref[theirs, rows, :])
    ghosts = []
    for t in range(count):
        cosine, sine = cos_ref[t], sin_ref[t]
        first = (row == 2) | (row == 3)
        other = (row == 4) | (row == 5)
        mate = jnp.where(first, pltpu.roll(low[t], 6, 0), pltpu.roll(low[t], 2, 0))
        turn = jnp.where(first, -sine, sine)
        a = jnp.where(first | other, cosine * low[t] + turn * mate, low[t])
        first = row < 2
        mate = jnp.where(first, pltpu.roll(high[t], 6, 0), pltpu.roll(high[t], 2, 0))
        turn = jnp.where(first, -sine, sine)
        b = jnp.where(row < 4, cosine * high[t] + turn * mate, high[t])
        ghosts.append((a, b))
    return ghosts


def keep_ghosts(lon, ghosts, line_ref, column_ref):
    for t in range(LANE_TILES):
        cols = slice(t * LANES, (t + 1) * LANES)
        line_ref[0:8, cols], line_ref[8:16, cols] = ghosts[t]

    def put_column():
        shape = (ROWS, LANES)
        diagonal = lane_of(shape) == row_of(shape)
        for f in range(FIELDS):
            values = jnp.broadcast_to(ghosts[LANE_TILES][f // 8][f % 8 : f % 8 + 1, :], shape)
            column = jnp.sum(jnp.where(diagonal, values, 0.0), axis=1, keepdims=True)
            column_ref[f] = jnp.broadcast_to(column, shape)

    pl.when((lon == 0) | (lon == 7))(put_column)


def tendency(work_ref, metric_ref, rb, k, emit, tile=None, ghosts=None):
    low = rb * 8
    rows = slice(low, low + 8)
    whole = tile is None
    cols = slice(0, COLS) if whole else slice(tile * LANES, (tile + 1) * LANES)
    shape = (8, cols.stop - cols.start)
    row = row_of(shape)
    lane = lane_of(shape)
    metric = metric_ref[rows, :]
    if whole:
        metric = jnp.concatenate([metric] * LANE_TILES, axis=1)
    square = metric * metric
    centre_weight = 4.0 + 2.0 * square
    radial = 0.5 if k == 0 else -0.5

    def value(c):
        return work_ref[2 * c + k, rows, cols]

    def beside(f, step):
        start = (tile + step) % LANE_TILES * LANES
        return work_ref[f, rows, start : start + LANES]

    def coefficients(c):
        return radial * value(c), 0.5 * value(c + 1), (0.5 * metric) * value(c + 2)

    flow_by = coefficients(0)
    field_by = coefficients(3)

    def parts(c):
        f = 2 * c + k
        centre = value(c)
        across = work_ref[2 * c + 1 - k, rows, cols]
        before = work_ref[f, (low - 1) % ROWS : (low - 1) % ROWS + 1, cols]
        after = work_ref[f, (low + 8) % ROWS : (low + 8) % ROWS + 1, cols]
        if ghosts is not None:
            (lat, lon), line_ref, column_ref = ghosts
            if rb == 0:
                before = jnp.where(lat == 0, line_ref[f : f + 1, cols], before)
            if rb == CT // 8 - 1:
                after = jnp.where(lat == NT // CT - 1, line_ref[f : f + 1, cols], after)
        north = jnp.where(row == 0, jnp.broadcast_to(before, shape), pltpu.roll(centre, 1, 0))
        south = jnp.where(row == 7, jnp.broadcast_to(after, shape), pltpu.roll(centre, 7, 0))
        west = pltpu.roll(centre, 1, 1)
        east = pltpu.roll(centre, shape[1] - 1, 1)
        if tile == 0:
            west = jnp.where(lane == 0, jnp.where(lon == 0, column_ref[f, rows, :], pltpu.roll(beside(f, -1), 1, 1)), west)
            east = jnp.where(lane == LANES - 1, pltpu.roll(beside(f, 1), LANES - 1, 1), east)
        elif tile is not None:
            west = jnp.where(lane == 0, pltpu.roll(beside(f, -1), 1, 1), west)
            east = jnp.where(lane == LANES - 1, pltpu.roll(beside(f, 1), LANES - 1, 1), east)
            east = jnp.where((lane == CP - LAST - 1) & (lon == 7), column_ref[f, rows, :], east)
        grad_t = south - north
        grad_p = east - west
        laplace = across + (south + north) + square * (east + west) - centre_weight * centre
        return across, grad_t, grad_p, laplace

    def along(by, p):
        return by[0] * p[0] + by[1] * p[1] + by[2] * p[2]

    for c in range(3):
        p = parts(c)
        u_flow, u_field, u_laplace = along(flow_by, p), along(field_by, p), p[3]
        p = parts(c + 3)
        velocity = along(field_by, p) - u_flow + viscosity * u_laplace
        if c == 0:
            velocity = velocity + buoyancy * value(6)
        emit(c, velocity)
        emit(c + 3, u_field - along(flow_by, p) + resistivity * p[3])
    p = parts(6)
    emit(6, conduction * p[3] - along(flow_by, p) + gradient * value(0))


def inner_kernel(factor, metric_ref, full_ref, now_ref, next_ref):
    for rb in range(ROWS // 8):
        rows = slice(rb * 8, rb * 8 + 8)
        for k in range(2):

            def emit(c, value):
                next_ref[2 * c + k, rows, :] = full_ref[2 * c + k, rows, :] + factor * value

            tendency(now_ref, metric_ref, rb, k, emit)


def first_inner_kernel(metric_ref, full_ref, next_ref):
    inner_kernel(time_step / 2, metric_ref, full_ref, full_ref, next_ref)


def put_rim(place, inner_ref, row_ref, column_ref, now_ref):
    lat, lon = place
    now_ref[...] = inner_ref[...]

    def put_row(rb):
        now_ref[:, rb * 8 : rb * 8 + 8, :] = row_ref[...]

    def put_column(tile):
        now_ref[:, :, tile * LANES : (tile + 1) * LANES] = column_ref[...]

    pl.when(lat == 0)(lambda: put_row(0))
    pl.when(lat == NT // CT - 1)(lambda: put_row(CT // 8 - 1))
    pl.when(lon == 0)(lambda: put_column(0))
    pl.when(lon == 7)(lambda: put_column(LANE_TILES - 1))


def next_inner_kernel(factor, aux_ref, metric_ref, full_ref, inner_ref, row_ref, column_ref, now_ref, next_ref):
    put_rim(place_of(aux_ref), inner_ref, row_ref, column_ref, now_ref)
    inner_kernel(factor, metric_ref, full_ref, now_ref, next_ref)


def on_rim(place, rb, t):
    lat, lon = place
    in_row = {0: lat == 0, CT // 8 - 1: lat == NT // CT - 1}.get(rb, False)
    in_column = {0: lon == 0, LANE_TILES - 1: lon == 7}.get(t, False)
    return in_row, in_column


def donor_kernel(aux_ref, inner_ref, index_ref, weight_ref, total_ref):
    place = place_of(aux_ref)
    totals = [None] * FIELDS

    def block_of(f, rb, t):
        return inner_ref[f, rb * 8 : rb * 8 + 8, t * LANES : (t + 1) * LANES]

    for t in range(LANE_TILES):
        for rb in range(CT // 8):
            weight = weight_ref[rb * LANE_TILES + t]
            for here in on_rim(place, rb, t):
                if here is not False:
                    weight = jnp.where(here, 0.0, weight)
            add_donors(totals, block_of, index_ref[t], weight, rb, t)
    for f in range(FIELDS):
        total_ref[f] = totals[f]


def redo_rim(place, now_ref, metric_ref, line_ref, column_ref, blocks, store):
    lat, lon = place

    def redo(rbs, tile):
        cols = slice(0, COLS) if tile is None else slice(tile * LANES, (tile + 1) * LANES)
        for rb in rbs:
            for k in range(2):

                def emit(c, value):
                    store(2 * c + k, slice(rb * 8, rb * 8 + 8), cols, value)

                tendency(now_ref, metric_ref, rb, k, emit, tile, (place, line_ref, column_ref))

    pl.when(lat == 0)(lambda: redo([0], None))
    pl.when(lat == NT // CT - 1)(lambda: redo([CT // 8 - 1], None))
    pl.when(lon == 0)(lambda: redo(range(blocks), 0))
    pl.when(lon == 7)(lambda: redo(range(blocks), LANE_TILES - 1))


def rim_kernel(
    factor, aux_ref, share_ref, other_ref, cos_ref, sin_ref, metric_ref, index_ref, weight_ref, total_ref, full_ref, now_ref,
    row_ref, side_ref, packet_ref, line_ref, column_ref, sum_ref,
):
    place = place_of(aux_ref)
    lat, lon = place
    keep_ghosts(lon, turned_ghosts(share_ref, other_ref, cos_ref, sin_ref), line_ref, column_ref)
    sum_ref[...] = total_ref[...]

    def store(f, rows, cols, value):
        value = full_ref[f, rows, cols] + factor * value
        if cols.stop - cols.start == COLS:
            row_ref[f] = value
        else:
            side_ref[f, rows, :] = value

    redo_rim(place, now_ref, metric_ref, line_ref, column_ref, ROWS // 8, store)

    def add(blocks, block_of, skip):
        totals = [sum_ref[f] for f in range(FIELDS)]
        for rb, t in blocks:
            weight = weight_ref[rb * LANE_TILES + t]
            if skip and on_rim(place, rb, t)[1] is not False:
                weight = jnp.where(on_rim(place, rb, t)[1], 0.0, weight)
            add_donors(totals, block_of, index_ref[t], weight, rb, t)
        for f in range(FIELDS):
            sum_ref[f] = totals[f]

    def add_row(rb):
        blocks = [(rb, t) for t in range(LANE_TILES)]
        add(blocks, lambda f, rb, t: row_ref[f, :, t * LANES : (t + 1) * LANES], True)

    def add_side(t):
        blocks = [(rb, t) for rb in range(CT // 8)]
        add(blocks, lambda f, rb, t: side_ref[f, rb * 8 : rb * 8 + 8, :], False)

    pl.when(lat == 0)(lambda: add_row(0))
    pl.when(lat == NT // CT - 1)(lambda: add_row(CT // 8 - 1))
    pl.when(lon == 0)(lambda: add_side(0))
    pl.when(lon == 7)(lambda: add_side(LANE_TILES - 1))
    packet_ref[...] = packed_rows([sum_ref[f] for f in range(FIELDS)])


def last_inner_kernel(
    aux_ref, metric_ref, full_ref, second_ref, third_ref, inner_ref, row_ref, column_ref, fourth_ref, base_ref, out_ref
):
    put_rim(place_of(aux_ref), inner_ref, row_ref, column_ref, fourth_ref)
    for rb in range(CT // 8):
        rows = slice(rb * 8, rb * 8 + 8)
        for k in range(2):

            def emit(c, value):
                f = 2 * c + k
                base = second_ref[f, rows, :] + 2.0 * third_ref[f, rows, :] + fourth_ref[f, rows, :] - full_ref[f, rows, :]
                base = (1.0 / 3.0) * base
                base_ref[f, rows, :] = base
                out_ref[f, rows, :] = base + (time_step / 6) * value

            tendency(fourth_ref, metric_ref, rb, k, emit)


def last_rim_kernel(
    aux_ref, share_ref, other_ref, cos_ref, sin_ref, metric_ref, base_ref, inner_ref, now_ref,
    out_ref, line_ref, column_ref,
):
    place = place_of(aux_ref)
    keep_ghosts(place[1], turned_ghosts(share_ref, other_ref, cos_ref, sin_ref), line_ref, column_ref)
    for f in range(FIELDS):
        out_ref[f] = inner_ref[f, :, 0:CP]

    def store(f, rows, cols, value):
        cols = slice(cols.start, min(cols.stop, CP))
        out = base_ref[f, rows, cols] + (time_step / 6) * value[:, : cols.stop - cols.start]
        out_ref[f, rows, cols] = out

    redo_rim(place, now_ref, metric_ref, line_ref, column_ref, CT // 8, store)


def call(kernel, ins, outs, scratch=(), cost=0, left=()):
    vmem = pl.BlockSpec(memory_space=pltpu.VMEM)
    hbm = pl.BlockSpec(memory_space=pltpu.HBM)
    shapes = tuple(jax.ShapeDtypeStruct(s, d) for s, d in outs)
    ins = [pltpu.with_memory_space_constraint(a, pltpu.HBM) if i in left else a for i, a in enumerate(ins)]
    return pl.pallas_call(
        kernel,
        out_shape=shapes,
        in_specs=[hbm if i in left else vmem for i in range(len(ins))],
        out_specs=(vmem,) * len(outs),
        scratch_shapes=list(scratch),
        compiler_params=pltpu.CompilerParams(vmem_limit_bytes=VMEM_LIMIT),
        cost_estimate=pl.CostEstimate(flops=cost * 1000, bytes_accessed=cost, transcendentals=0) if cost else None,
    )(*ins)


def coordinates(axes):
    points = [()]
    for a in axes:
        points = [q + (i,) for q in points for i in range(SIZES[a])]
    return points


def permute(value, axes, move):
    points = coordinates(axes)
    place = {q: i for i, q in enumerate(points)}
    pairs = []
    for q in points:
        to = move(q)
        if to is not None:
            pairs.append((place[q], place[to]))
    return lax.ppermute(value, axes if len(axes) > 1 else axes[0], pairs)


def within(value, axes):
    return permute(value, axes, lambda q: (q[0], 1 - q[1]))


def between(value, axes):
    count = SIZES[axes[0]]
    return permute(value, axes, lambda q: ((q[0] + 1) % count, 0) if q[1] == 1 else ((q[0] - 1) % count, 1))


def swap_packets(packet):
    same = permute(packet, ("panel", "xh"), lambda q: (1 - q[0], q[1]))
    other = permute(packet, ("panel", "xh"), lambda q: (1 - q[0], 1 - q[1]))
    second = lane_of(packet.shape) >= 64
    return jnp.where(second == (lax.axis_index("xh") == 1), same, other)


def spread_packets(pair):
    count = SIZES["z"] * SIZES["y"]
    return lax.all_to_all(jnp.broadcast_to(pair[None], (count,) + pair.shape), ("y", "z"), 0, 0)


def other_core(value):
    return permute(value, ("core",), lambda q: (1 - q[0],))


def on_device(state, pack_cell, pack_frac, ns_source, we_source, ns_turn, we_turn):
    f32 = jnp.float32
    tile = state.reshape(FIELDS, CT, CP)
    lat = lax.axis_index(LAT)
    lon = lax.axis_index(LON)
    panel = lax.axis_index("panel")
    flags = jnp.broadcast_to(jnp.stack([lat, lon, panel] + [panel] * 5).astype(jnp.int32)[:, None], (8, LANES))
    raw = [pack_cell.reshape(1, SLOTS), pack_frac.reshape(2, SLOTS), ns_source, we_source, ns_turn, we_turn]
    vreg = (8, LANES)
    packed = ((16, LANES), f32)
    whole = ((FIELDS, ROWS, COLS), f32)
    lat_message = ((8, 8, COLS), f32)
    lon_message = ((CT, LANES), f32)
    tile, aux, packet, lon_inner, lon_cross, index, weight = call(
        open_kernel,
        [flags, tile] + raw,
        [
            ((FIELDS, CT, CP), f32),
            ((8, COLS), f32),
            packed,
            lon_message,
            lon_message,
            ((LANE_TILES,) + vreg, jnp.int32),
            ((3 * LANE_TILES,) + vreg, f32),
        ],
        scratch=[pltpu.VMEM(a.shape, a.dtype) for a in raw] + [pltpu.SemaphoreType.DMA((len(raw) + 1,))],
        left=range(1, 8),
    )
    lon_inner = within(lon_inner, LON)
    lon_cross = between(lon_cross, LON)
    pair = swap_packets(packet)
    lat_inner, lat_cross = call(lat_kernel, [aux, tile, lon_inner, lon_cross], [lat_message] * 2, cost=8_000_000)
    lat_inner = within(lat_inner, LAT)
    lat_cross = between(lat_cross, LAT)
    donors = spread_packets(pair)
    donors, lat_inner, lat_cross = lax.optimization_barrier((donors, lat_inner, lat_cross))
    points = (LANE_TILES + 1,) + vreg
    full, slot, where, cosine, sine, metric, column = call(
        frame_kernel,
        [aux, tile, lat_inner, lat_cross, lon_inner, lon_cross],
        [whole, (points, jnp.int32), (points, jnp.int32), (points, f32), (points, f32), ((ROWS, LANES), f32), ((16, LANES), jnp.int32)],
    )
    lists = [slot, where, other_core(column)]
    kept = [pltpu.VMEM((16, COLS), f32), pltpu.VMEM((FIELDS, ROWS, LANES), f32)]

    def ghost_tables(donors):
        (share,) = call(pick_kernel, [aux, donors] + lists, [((LANE_TILES + 2, 16, LANES), f32)])
        return [aux, share, other_core(share), cosine, sine, metric]

    row, side = ((FIELDS, 8, COLS), f32), ((FIELDS, ROWS, LANES), f32)
    totals = ((FIELDS,) + vreg, f32)
    states = [full]
    for factor in (time_step / 2, time_step / 2, time_step):
        if len(states) == 1:
            (inner,) = call(first_inner_kernel, [metric, full], [whole], cost=2_000_000)
            donors, inner = lax.optimization_barrier((donors, inner))
        else:
            pair = swap_packets(packet)
            now, inner = call(
                functools.partial(next_inner_kernel, factor), [aux, metric, full, inner] + rim, [whole, whole], cost=2_000_000
            )
            states[-1] = now
            pair, inner = lax.optimization_barrier((pair, inner))
            donors = spread_packets(pair)
        tables = ghost_tables(donors)
        (sums,) = call(donor_kernel, [aux, inner, index, weight], [totals], cost=500_000)
        *rim, packet = call(
            functools.partial(rim_kernel, factor),
            tables + [index, weight, sums, full, states[-1]],
            [row, side, packed],
            scratch=kept + [pltpu.VMEM(*totals)],
        )
        states.append(None)
    pair = swap_packets(packet)
    inner_shape = ((FIELDS, CT, COLS), f32)
    states[-1], base, inner = call(
        last_inner_kernel, [aux, metric] + states[:-1] + [inner] + rim, [whole, inner_shape, inner_shape], cost=2_000_000
    )
    pair, inner = lax.optimization_barrier((pair, inner))
    (result,) = call(
        last_rim_kernel,
        ghost_tables(spread_packets(pair)) + [base, inner, states[-1]],
        [((FIELDS, CT, CP), f32)],
        scratch=kept,
    )
    return result.reshape(state.shape)


def solution(mesh):
    fine = Mesh(mesh.devices.reshape(tuple(SIZES[a] for a in AXES)), AXES)
    return jax.shard_map(
        on_device,
        mesh=fine,
        in_specs=(
            P("panel", None, None, LAT, LON),
            P("panel", LAT, LON, None),
            P("panel", None, LAT, LON, None),
            P(None, None, LON),
            P(None, None, LAT),
            P(None, None, LON),
            P(None, None, LAT),
        ),
        out_specs=P("panel", None, None, LAT, LON),
        check_vma=False,
    )
```

```python
import functools
import math

import jax
import jax.numpy as jnp
from jax import lax
from jax.experimental import pallas as pl
from jax.experimental.pallas import tpu as pltpu
from jax.sharding import Mesh, PartitionSpec as P

time_step = 0.25
viscosity = 0.1
resistivity = 0.08
conduction = 0.12
buoyancy = 0.5
gradient = 0.5

AXES = ("panel", "z", "core", "y", "xh")
SIZES = dict(zip(AXES, (2, 8, 2, 4, 2)))
LAT = ("z", "core")
LON = ("y", "xh")

FIELDS = 14
CT = 24
CP = 576
ROWS = 32
COLS = 640
HALO = 4
SLOTS = 48
NT = 384
LANES = 128
TILES = 128
LANE_TILES = COLS // LANES
LAST = COLS - LANES
SPARE = 68
VMEM_LIMIT = 24 * 1024 * 1024


def lane_of(shape):
    return lax.broadcasted_iota(jnp.int32, shape, len(shape) - 1)


def row_of(shape):
    return lax.broadcasted_iota(jnp.int32, shape, len(shape) - 2)


def lane_gather(block, index):
    return jnp.take_along_axis(block, index, axis=1, mode="promise_in_bounds")


def add_donors(totals, block_of, index, weight, rb, t):
    for f in range(FIELDS):
        term = weight * lane_gather(block_of(f, rb, t), index)
        totals[f] = term if totals[f] is None else totals[f] + term


def packed_rows(totals):
    rows = [jnp.sum(total, axis=0, keepdims=True) for total in totals]
    rows += [jnp.zeros((1, LANES), jnp.float32)] * (16 - FIELDS)
    packet = jnp.concatenate(rows, axis=0)
    return packet + pltpu.roll(packet, 64, 1)


def build_packet(block_of, index_ref, weight_ref):
    totals = [None] * FIELDS
    for t in range(LANE_TILES):
        for rb in range(CT // 8):
            add_donors(totals, block_of, index_ref[t], weight_ref[rb * LANE_TILES + t], rb, t)
    return packed_rows(totals)


def state_block(state_ref, f, rb, t):
    rows = slice(rb * 8, rb * 8 + 8)
    if t < LANE_TILES - 1:
        return state_ref[f, rows, t * LANES : (t + 1) * LANES]
    half = state_ref[f, rows, LAST:CP]
    return jnp.concatenate([half, jnp.zeros((8, LANES - 64), jnp.float32)], axis=1)


def place_of(aux_ref):
    return aux_ref[7, 0].astype(jnp.int32), aux_ref[7, LANES].astype(jnp.int32)


def open_kernel(
    flags_ref, state_hbm, cell_hbm, frac_hbm, ns_source_hbm, we_source_hbm, ns_turn_hbm, we_turn_hbm,
    state_ref, aux_ref, packet_ref, inner_ref, cross_ref, index_ref, weight_ref,
    cell_ref, frac_ref, ns_source_ref, we_source_ref, ns_turn_ref, we_turn_ref, semaphores,
):
    sources = (cell_hbm, frac_hbm, ns_source_hbm, we_source_hbm, ns_turn_hbm, we_turn_hbm, state_hbm)
    targets = (cell_ref, frac_ref, ns_source_ref, we_source_ref, ns_turn_ref, we_turn_ref, state_ref)
    copies = [pltpu.make_async_copy(sources[i], targets[i], semaphores.at[i]) for i in range(len(sources))]
    for copy in copies:
        copy.start()
    for copy in copies[:-1]:
        copy.wait()
    panel = flags_ref[2, 0]
    far_south = flags_ref[0, 0] >= NT // CT - 2
    far_east = flags_ref[1, 0] == 7
    aux_ref[...] = jnp.zeros((8, COLS), jnp.float32)
    for i, (table, far) in enumerate(
        ((ns_source_ref, far_south), (ns_turn_ref, far_south), (we_source_ref, far_east), (we_turn_ref, far_east))
    ):
        both = table[panel].astype(jnp.float32)
        aux_ref[i : i + 1, 0 : both.shape[1]] = jnp.where(far, both[1:2, :], both[0:1, :])
    aux_ref[7:8, 0:LANES] = flags_ref[0:1, :].astype(jnp.float32)
    aux_ref[7:8, LANES : 2 * LANES] = flags_ref[1:2, :].astype(jnp.float32)
    shape = (8, LANES)
    lane = lane_of(shape)
    row = row_of(shape)
    copies[-1].wait()
    for rb in range(CT // 8):
        west = jnp.zeros(shape, jnp.float32)
        east = jnp.zeros(shape, jnp.float32)
        for f in range(FIELDS):
            first = state_block(state_ref, f, rb, 0)
            last = state_block(state_ref, f, rb, LANE_TILES - 1)
            here = (lane >= 8 * f) & (lane < 8 * f + HALO)
            west = jnp.where(here, pltpu.roll(first, 8 * f, 1) if f else first, west)
            east = jnp.where(here, pltpu.roll(last, (8 * f - 60) % LANES, 1), east)
        if rb == 0:
            here = (lane >= 112) & (lane < 112 + HALO)
            west = jnp.where(here, pltpu.roll(aux_ref[:, 0:LANES], 112, 1), west)
            east = jnp.where(here, pltpu.roll(aux_ref[:, LAST:COLS], 112 - 60, 1), east)
        rows = slice(rb * 8, rb * 8 + 8)
        inner_ref[rows, :], cross_ref[rows, :] = ordered(flags_ref[1, 0], east, west)

    def doubled(line):
        line = jnp.concatenate([line, jnp.zeros((1, LANES - SLOTS), jnp.float32)], axis=1)
        line = jnp.broadcast_to(line, shape)
        return jnp.where(lane < 64, line, pltpu.roll(line, 64, 1))

    cell = doubled(cell_ref[...].astype(jnp.float32))
    frac_u = doubled(frac_ref[0:1, :])
    frac_v = doubled(frac_ref[1:2, :])
    lat_off = jnp.floor((cell + 0.5) * (1.0 / (CP - 1)))
    lon_off = cell - lat_off * (CP - 1)
    lat_off = lat_off.astype(jnp.int32)
    second = lane >= 64
    column = lon_off.astype(jnp.int32) + second.astype(jnp.int32)
    used = (lane & 63) < SLOTS
    along = jnp.where(second, frac_v, 1.0 - frac_v)
    for t in range(LANE_TILES):
        local = column - t * LANES
        inside = used & (local >= 0) & (local < LANES)
        index_ref[t] = jnp.where(inside, local, 0)
        for rb in range(CT // 8):
            here = row + rb * 8
            down = jnp.where(here == lat_off, 1.0 - frac_u, jnp.where(here == lat_off + 1, frac_u, 0.0))
            weight_ref[rb * LANE_TILES + t] = jnp.where(inside, down * along, 0.0)
    packet_ref[...] = build_packet(functools.partial(state_block, state_ref), index_ref, weight_ref)


def ordered(flag, inner, cross):
    first = (flag & 1) == 0
    return jnp.where(first, inner, cross), jnp.where(first, cross, inner)


def outer_rows(from_south, from_north, k, row):
    if k == 0:
        return jnp.where(row < HALO, from_south, pltpu.roll(from_north, HALO, 0))
    return jnp.where(row < HALO, pltpu.roll(from_south, HALO, 0), from_north)


def column_list(aux_ref, lat_inner_ref, lat_cross_ref):
    lane = lane_of((8, LANES))
    block = aux_ref[:, 0:LANES]
    south, north = ordered(place_of(aux_ref)[0], lat_inner_ref[0, :, LAST:COLS], lat_cross_ref[0, :, LAST:COLS])
    block = jnp.where((lane >= CT) & (lane < CT + HALO), pltpu.roll(south, (CT - SPARE) % LANES, 1), block)
    return jnp.where((lane >= ROWS - HALO) & (lane < ROWS), pltpu.roll(north, (8 - SPARE) % LANES, 1), block)


def donor_places(source):
    whole = jnp.floor((source + 0.5) * (1.0 / SLOTS))
    tile = whole.astype(jnp.int32)
    return (source - whole * SLOTS).astype(jnp.int32) + 64 * (tile & 1), tile // 2


def lat_kernel(aux_ref, state_ref, lon_inner_ref, lon_cross_ref, inner_ref, cross_ref):
    shape = (8, LANES)
    lane = lane_of(shape)
    row = row_of(shape)
    lat, lon = place_of(aux_ref)
    first_core = (lat & 1) == 0

    def block(f, rb, t):
        value = state_block(state_ref, f, rb, t)
        if t < LANE_TILES - 1:
            return value
        rows = slice(rb * 8, rb * 8 + 8)
        return with_columns(value, *ordered(lon, lon_inner_ref[rows, :], lon_cross_ref[rows, :]), f, lane)

    for c in range(7):
        for t in range(LANE_TILES):
            cols = slice(t * LANES, (t + 1) * LANES)
            top = [block(2 * c + k, 0, t) for k in range(2)]
            end = [block(2 * c + k, CT // 8 - 1, t) for k in range(2)]
            north = jnp.where(row < HALO, top[0], pltpu.roll(top[1], HALO, 0))
            south = jnp.where(row < HALO, pltpu.roll(end[0], HALO, 0), end[1])
            inner = jnp.where(first_core, south, north)
            cross = jnp.where(first_core, north, south)
            if c == 0 and t == LANE_TILES - 1:
                here = (lane >= SPARE) & (lane < SPARE + CT)
                lists = pltpu.roll(aux_ref[:, 0:LANES], SPARE, 1)
                inner, cross = jnp.where(here, lists, inner), jnp.where(here, lists, cross)
            inner_ref[c, :, cols] = inner
            cross_ref[c, :, cols] = cross


def with_columns(block, from_east, from_west, f, lane):
    block = jnp.where((lane >= 64) & (lane < 64 + HALO), pltpu.roll(from_east, (64 - 8 * f) % LANES, 1), block)
    return jnp.where(lane >= LANES - HALO, pltpu.roll(from_west, (124 - 8 * f) % LANES, 1), block)


def frame_kernel(
    aux_ref, state_ref, lat_inner_ref, lat_cross_ref, lon_inner_ref, lon_cross_ref,
    full_ref, slot_ref, tile_ref, cos_ref, sin_ref, metric_ref, column_ref,
):
    shape = (8, LANES)
    lat, lon = place_of(aux_ref)
    lane = lane_of(shape)
    row = row_of(shape)
    for rb in range(ROWS // 8):
        rows = slice(rb * 8, rb * 8 + 8)
        for f in range(FIELDS):
            c, k = f // 2, f % 2
            for t in range(LANE_TILES):
                cols = slice(t * LANES, (t + 1) * LANES)
                if rb < CT // 8:
                    block = state_block(state_ref, f, rb, t)
                    if t == LANE_TILES - 1:
                        sides = ordered(lon, lon_inner_ref[rows, :], lon_cross_ref[rows, :])
                        block = with_columns(block, *sides, f, lane)
                else:
                    south, north = ordered(lat, lat_inner_ref[c, :, cols], lat_cross_ref[c, :, cols])
                    block = outer_rows(south, north, k, row)
                    if t == LANE_TILES - 1:
                        block = jnp.where((lane >= SPARE) & (lane < LANES - HALO), 0.0, block)
                full_ref[f, rows, cols] = block
    for t in range(LANE_TILES + 1):
        if t < LANE_TILES:
            block = aux_ref[:, t * LANES : (t + 1) * LANES]
            if t == LANE_TILES - 1:
                east, west = ordered(lon, lon_inner_ref[0:8, :], lon_cross_ref[0:8, :])
                block = jnp.where((lane >= 64) & (lane < 64 + HALO), pltpu.roll(east, (64 - 112) % LANES, 1), block)
                block = jnp.where(lane >= LANES - HALO, pltpu.roll(west, 124 - 112, 1), block)
            source = jnp.broadcast_to(block[0:1, :], shape)
            angle = jnp.broadcast_to(block[1:2, :], shape)
        else:
            block = column_list(aux_ref, lat_inner_ref, lat_cross_ref)
            source = jnp.broadcast_to(block[2:3, :], shape)
            angle = jnp.broadcast_to(block[3:4, :], shape)
        slot_ref[t], tile_ref[t] = donor_places(source)
        if t == LANE_TILES:
            column_ref[0:8, :], column_ref[8:16, :] = donor_places(source)
        cos_ref[t] = jnp.cos(angle)
        sin_ref[t] = jnp.sin(angle)
    line = row_of((ROWS, LANES))
    line = jnp.where(line >= ROWS - HALO, line - ROWS, line) + lat * CT
    theta = math.pi / 4 + (line.astype(jnp.float32) + 0.5) * ((math.pi / 2) / NT)
    metric_ref[...] = 1.0 / jnp.sin(theta)


def pick_kernel(aux_ref, donor_ref, slot_ref, tile_ref, other_ref, out_ref):
    mine = 4 * (place_of(aux_ref)[0] & 1)
    count = LANE_TILES + 1
    tables = [(slot_ref[t], tile_ref[t]) for t in range(count)] + [(other_ref[0:8, :], other_ref[8:16, :])]
    for t, (slots, pairs) in enumerate(tables):
        pairs = pairs - mine
        low = jnp.zeros((8, LANES), jnp.float32)
        high = jnp.zeros((8, LANES), jnp.float32)
        for v in range(TILES // 4):
            here = pairs == v % 8 * 8 + v // 8
            low = jnp.where(here, lane_gather(donor_ref[v, 0:8, :], slots), low)
            high = jnp.where(here, lane_gather(donor_ref[v, 8:16, :], slots), high)
        out_ref[t, 0:8, :] = low
        out_ref[t, 8:16, :] = high


def turned_ghosts(share_ref, other_ref, cos_ref, sin_ref):
    shape = (8, LANES)
    row = row_of(shape)
    count = LANE_TILES + 1
    low, high = [], []
    for t in range(count):
        theirs = t if t < LANE_TILES else count
        for out, rows in ((low, slice(0, 8)), (high, slice(8, 16))):
            out.append(share_ref[t, rows, :] + other_ref[theirs, rows, :])
    ghosts = []
    for t in range(count):
        cosine, sine = cos_ref[t], sin_ref[t]
        first = (row == 2) | (row == 3)
        other = (row == 4) | (row == 5)
        mate = jnp.where(first, pltpu.roll(low[t], 6, 0), pltpu.roll(low[t], 2, 0))
        turn = jnp.where(first, -sine, sine)
        a = jnp.where(first | other, cosine * low[t] + turn * mate, low[t])
        first = row < 2
        mate = jnp.where(first, pltpu.roll(high[t], 6, 0), pltpu.roll(high[t], 2, 0))
        turn = jnp.where(first, -sine, sine)
        b = jnp.where(row < 4, cosine * high[t] + turn * mate, high[t])
        ghosts.append((a, b))
    return ghosts


def keep_ghosts(lon, ghosts, line_ref, column_ref):
    for t in range(LANE_TILES):
        cols = slice(t * LANES, (t + 1) * LANES)
        line_ref[0:8, cols], line_ref[8:16, cols] = ghosts[t]

    def put_column():
        shape = (ROWS, LANES)
        diagonal = lane_of(shape) == row_of(shape)
        for f in range(FIELDS):
            values = jnp.broadcast_to(ghosts[LANE_TILES][f // 8][f % 8 : f % 8 + 1, :], shape)
            column = jnp.sum(jnp.where(diagonal, values, 0.0), axis=1, keepdims=True)
            column_ref[f] = jnp.broadcast_to(column, shape)

    pl.when((lon == 0) | (lon == 7))(put_column)


def tendency(work_ref, metric_ref, rb, k, emit, tile=None, ghosts=None):
    low = rb * 8
    rows = slice(low, low + 8)
    whole = tile is None
    cols = slice(0, COLS) if whole else slice(tile * LANES, (tile + 1) * LANES)
    shape = (8, cols.stop - cols.start)
    row = row_of(shape)
    lane = lane_of(shape)
    metric = metric_ref[rows, :]
    if whole:
        metric = jnp.concatenate([metric] * LANE_TILES, axis=1)
    square = metric * metric
    centre_weight = 4.0 + 2.0 * square
    radial = 0.5 if k == 0 else -0.5

    def value(c):
        return work_ref[2 * c + k, rows, cols]

    def beside(f, step):
        start = (tile + step) % LANE_TILES * LANES
        return work_ref[f, rows, start : start + LANES]

    def coefficients(c):
        return radial * value(c), 0.5 * value(c + 1), (0.5 * metric) * value(c + 2)

    flow_by = coefficients(0)
    field_by = coefficients(3)

    def parts(c):
        f = 2 * c + k
        centre = value(c)
        across = work_ref[2 * c + 1 - k, rows, cols]
        before = work_ref[f, (low - 1) % ROWS : (low - 1) % ROWS + 1, cols]
        after = work_ref[f, (low + 8) % ROWS : (low + 8) % ROWS + 1, cols]
        if ghosts is not None:
            (lat, lon), line_ref, column_ref = ghosts
            if rb == 0:
                before = jnp.where(lat == 0, line_ref[f : f + 1, cols], before)
            if rb == CT // 8 - 1:
                after = jnp.where(lat == NT // CT - 1, line_ref[f : f + 1, cols], after)
        north = jnp.where(row == 0, jnp.broadcast_to(before, shape), pltpu.roll(centre, 1, 0))
        south = jnp.where(row == 7, jnp.broadcast_to(after, shape), pltpu.roll(centre, 7, 0))
        west = pltpu.roll(centre, 1, 1)
        east = pltpu.roll(centre, shape[1] - 1, 1)
        if tile == 0:
            west = jnp.where(lane == 0, jnp.where(lon == 0, column_ref[f, rows, :], pltpu.roll(beside(f, -1), 1, 1)), west)
            east = jnp.where(lane == LANES - 1, pltpu.roll(beside(f, 1), LANES - 1, 1), east)
        elif tile is not None:
            west = jnp.where(lane == 0, pltpu.roll(beside(f, -1), 1, 1), west)
            east = jnp.where(lane == LANES - 1, pltpu.roll(beside(f, 1), LANES - 1, 1), east)
            east = jnp.where((lane == CP - LAST - 1) & (lon == 7), column_ref[f, rows, :], east)
        grad_t = south - north
        grad_p = east - west
        laplace = across + (south + north) + square * (east + west) - centre_weight * centre
        return across, grad_t, grad_p, laplace

    def along(by, p):
        return by[0] * p[0] + by[1] * p[1] + by[2] * p[2]

    for c in range(3):
        p = parts(c)
        u_flow, u_field, u_laplace = along(flow_by, p), along(field_by, p), p[3]
        p = parts(c + 3)
        velocity = along(field_by, p) - u_flow + viscosity * u_laplace
        if c == 0:
            velocity = velocity + buoyancy * value(6)
        emit(c, velocity)
        emit(c + 3, u_field - along(flow_by, p) + resistivity * p[3])
    p = parts(6)
    emit(6, conduction * p[3] - along(flow_by, p) + gradient * value(0))


def inner_kernel(factor, metric_ref, full_ref, now_ref, next_ref):
    for rb in range(ROWS // 8):
        rows = slice(rb * 8, rb * 8 + 8)
        for k in range(2):

            def emit(c, value):
                next_ref[2 * c + k, rows, :] = full_ref[2 * c + k, rows, :] + factor * value

            tendency(now_ref, metric_ref, rb, k, emit)


def first_inner_kernel(metric_ref, full_ref, next_ref):
    inner_kernel(time_step / 2, metric_ref, full_ref, full_ref, next_ref)


def put_rim(place, inner_ref, row_ref, column_ref, now_ref):
    lat, lon = place
    now_ref[...] = inner_ref[...]

    def put_row(rb):
        now_ref[:, rb * 8 : rb * 8 + 8, :] = row_ref[...]

    def put_column(tile):
        now_ref[:, :, tile * LANES : (tile + 1) * LANES] = column_ref[...]

    pl.when(lat == 0)(lambda: put_row(0))
    pl.when(lat == NT // CT - 1)(lambda: put_row(CT // 8 - 1))
    pl.when(lon == 0)(lambda: put_column(0))
    pl.when(lon == 7)(lambda: put_column(LANE_TILES - 1))


def next_inner_kernel(factor, aux_ref, metric_ref, full_ref, inner_ref, row_ref, column_ref, now_ref, next_ref):
    put_rim(place_of(aux_ref), inner_ref, row_ref, column_ref, now_ref)
    inner_kernel(factor, metric_ref, full_ref, now_ref, next_ref)


def on_rim(place, rb, t):
    lat, lon = place
    in_row = {0: lat == 0, CT // 8 - 1: lat == NT // CT - 1}.get(rb, False)
    in_column = {0: lon == 0, LANE_TILES - 1: lon == 7}.get(t, False)
    return in_row, in_column


def donor_kernel(aux_ref, inner_ref, index_ref, weight_ref, total_ref):
    place = place_of(aux_ref)
    totals = [None] * FIELDS

    def block_of(f, rb, t):
        return inner_ref[f, rb * 8 : rb * 8 + 8, t * LANES : (t + 1) * LANES]

    for t in range(LANE_TILES):
        for rb in range(CT // 8):
            weight = weight_ref[rb * LANE_TILES + t]
            for here in on_rim(place, rb, t):
                if here is not False:
                    weight = jnp.where(here, 0.0, weight)
            add_donors(totals, block_of, index_ref[t], weight, rb, t)
    for f in range(FIELDS):
        total_ref[f] = totals[f]


def redo_rim(place, now_ref, metric_ref, line_ref, column_ref, blocks, store):
    lat, lon = place

    def redo(rbs, tile):
        cols = slice(0, COLS) if tile is None else slice(tile * LANES, (tile + 1) * LANES)
        for rb in rbs:
            for k in range(2):

                def emit(c, value):
                    store(2 * c + k, slice(rb * 8, rb * 8 + 8), cols, value)

                tendency(now_ref, metric_ref, rb, k, emit, tile, (place, line_ref, column_ref))

    pl.when(lat == 0)(lambda: redo([0], None))
    pl.when(lat == NT // CT - 1)(lambda: redo([CT // 8 - 1], None))
    pl.when(lon == 0)(lambda: redo(range(blocks), 0))
    pl.when(lon == 7)(lambda: redo(range(blocks), LANE_TILES - 1))


def rim_kernel(
    factor, aux_ref, share_ref, other_ref, cos_ref, sin_ref, metric_ref, index_ref, weight_ref, total_ref, full_ref, now_ref,
    row_ref, side_ref, packet_ref, line_ref, column_ref, sum_ref,
):
    place = place_of(aux_ref)
    lat, lon = place
    keep_ghosts(lon, turned_ghosts(share_ref, other_ref, cos_ref, sin_ref), line_ref, column_ref)
    sum_ref[...] = total_ref[...]

    def store(f, rows, cols, value):
        value = full_ref[f, rows, cols] + factor * value
        if cols.stop - cols.start == COLS:
            row_ref[f] = value
        else:
            side_ref[f, rows, :] = value

    redo_rim(place, now_ref, metric_ref, line_ref, column_ref, ROWS // 8, store)

    def add(blocks, block_of, skip):
        totals = [sum_ref[f] for f in range(FIELDS)]
        for rb, t in blocks:
            weight = weight_ref[rb * LANE_TILES + t]
            if skip and on_rim(place, rb, t)[1] is not False:
                weight = jnp.where(on_rim(place, rb, t)[1], 0.0, weight)
            add_donors(totals, block_of, index_ref[t], weight, rb, t)
        for f in range(FIELDS):
            sum_ref[f] = totals[f]

    def add_row(rb):
        blocks = [(rb, t) for t in range(LANE_TILES)]
        add(blocks, lambda f, rb, t: row_ref[f, :, t * LANES : (t + 1) * LANES], True)

    def add_side(t):
        blocks = [(rb, t) for rb in range(CT // 8)]
        add(blocks, lambda f, rb, t: side_ref[f, rb * 8 : rb * 8 + 8, :], False)

    pl.when(lat == 0)(lambda: add_row(0))
    pl.when(lat == NT // CT - 1)(lambda: add_row(CT // 8 - 1))
    pl.when(lon == 0)(lambda: add_side(0))
    pl.when(lon == 7)(lambda: add_side(LANE_TILES - 1))
    packet_ref[...] = packed_rows([sum_ref[f] for f in range(FIELDS)])


def last_inner_kernel(
    aux_ref, metric_ref, full_ref, second_ref, third_ref, inner_ref, row_ref, column_ref, fourth_ref, base_ref, out_ref
):
    put_rim(place_of(aux_ref), inner_ref, row_ref, column_ref, fourth_ref)
    for rb in range(CT // 8):
        rows = slice(rb * 8, rb * 8 + 8)
        for k in range(2):

            def emit(c, value):
                f = 2 * c + k
                base = second_ref[f, rows, :] + 2.0 * third_ref[f, rows, :] + fourth_ref[f, rows, :] - full_ref[f, rows, :]
                base = (1.0 / 3.0) * base
                base_ref[f, rows, :] = base
                out_ref[f, rows, :] = base + (time_step / 6) * value

            tendency(fourth_ref, metric_ref, rb, k, emit)


def last_rim_kernel(
    aux_ref, share_ref, other_ref, cos_ref, sin_ref, metric_ref, base_ref, inner_ref, now_ref,
    out_ref, line_ref, column_ref,
):
    place = place_of(aux_ref)
    keep_ghosts(place[1], turned_ghosts(share_ref, other_ref, cos_ref, sin_ref), line_ref, column_ref)
    for f in range(FIELDS):
        out_ref[f] = inner_ref[f, :, 0:CP]

    def store(f, rows, cols, value):
        cols = slice(cols.start, min(cols.stop, CP))
        out = base_ref[f, rows, cols] + (time_step / 6) * value[:, : cols.stop - cols.start]
        out_ref[f, rows, cols] = out

    redo_rim(place, now_ref, metric_ref, line_ref, column_ref, CT // 8, store)


def call(kernel, ins, outs, scratch=(), cost=0, left=()):
    vmem = pl.BlockSpec(memory_space=pltpu.VMEM)
    hbm = pl.BlockSpec(memory_space=pltpu.HBM)
    shapes = tuple(jax.ShapeDtypeStruct(s, d) for s, d in outs)
    ins = [pltpu.with_memory_space_constraint(a, pltpu.HBM) if i in left else a for i, a in enumerate(ins)]
    return pl.pallas_call(
        kernel,
        out_shape=shapes,
        in_specs=[hbm if i in left else vmem for i in range(len(ins))],
        out_specs=(vmem,) * len(outs),
        scratch_shapes=list(scratch),
        compiler_params=pltpu.CompilerParams(vmem_limit_bytes=VMEM_LIMIT),
        cost_estimate=pl.CostEstimate(flops=cost * 1000, bytes_accessed=cost, transcendentals=0) if cost else None,
    )(*ins)


def coordinates(axes):
    points = [()]
    for a in axes:
        points = [q + (i,) for q in points for i in range(SIZES[a])]
    return points


def permute(value, axes, move):
    points = coordinates(axes)
    place = {q: i for i, q in enumerate(points)}
    pairs = []
    for q in points:
        to = move(q)
        if to is not None:
            pairs.append((place[q], place[to]))
    return lax.ppermute(value, axes if len(axes) > 1 else axes[0], pairs)


def within(value, axes):
    return permute(value, axes, lambda q: (q[0], 1 - q[1]))


def between(value, axes):
    count = SIZES[axes[0]]
    return permute(value, axes, lambda q: ((q[0] + 1) % count, 0) if q[1] == 1 else ((q[0] - 1) % count, 1))


def swap_packets(packet):
    same = permute(packet, ("panel", "xh"), lambda q: (1 - q[0], q[1]))
    other = permute(packet, ("panel", "xh"), lambda q: (1 - q[0], 1 - q[1]))
    second = lane_of(packet.shape) >= 64
    return jnp.where(second == (lax.axis_index("xh") == 1), same, other)


def spread_packets(pair):
    count = SIZES["z"] * SIZES["y"]
    return lax.all_to_all(jnp.broadcast_to(pair[None], (count,) + pair.shape), ("y", "z"), 0, 0)


def other_core(value):
    return permute(value, ("core",), lambda q: (1 - q[0],))


def on_device(state, pack_cell, pack_frac, ns_source, we_source, ns_turn, we_turn):
    f32 = jnp.float32
    tile = state.reshape(FIELDS, CT, CP)
    lat = lax.axis_index(LAT)
    lon = lax.axis_index(LON)
    panel = lax.axis_index("panel")
    flags = jnp.broadcast_to(jnp.stack([lat, lon, panel] + [panel] * 5).astype(jnp.int32)[:, None], (8, LANES))
    raw = [pack_cell.reshape(1, SLOTS), pack_frac.reshape(2, SLOTS), ns_source, we_source, ns_turn, we_turn]
    vreg = (8, LANES)
    packed = ((16, LANES), f32)
    whole = ((FIELDS, ROWS, COLS), f32)
    lat_message = ((7, 8, COLS), f32)
    lon_message = ((CT, LANES), f32)
    tile, aux, packet, lon_inner, lon_cross, index, weight = call(
        open_kernel,
        [flags, tile] + raw,
        [
            ((FIELDS, CT, CP), f32),
            ((8, COLS), f32),
            packed,
            lon_message,
            lon_message,
            ((LANE_TILES,) + vreg, jnp.int32),
            ((3 * LANE_TILES,) + vreg, f32),
        ],
        scratch=[pltpu.VMEM(a.shape, a.dtype) for a in raw] + [pltpu.SemaphoreType.DMA((len(raw) + 1,))],
        left=range(1, 8),
    )
    lon_inner = within(lon_inner, LON)
    lon_cross = between(lon_cross, LON)
    pair = swap_packets(packet)
    lat_inner, lat_cross = call(lat_kernel, [aux, tile, lon_inner, lon_cross], [lat_message] * 2, cost=8_000_000)
    lat_inner = within(lat_inner, LAT)
    lat_cross = between(lat_cross, LAT)
    donors = spread_packets(pair)
    donors, lat_inner, lat_cross = lax.optimization_barrier((donors, lat_inner, lat_cross))
    points = (LANE_TILES + 1,) + vreg
    full, slot, where, cosine, sine, metric, column = call(
        frame_kernel,
        [aux, tile, lat_inner, lat_cross, lon_inner, lon_cross],
        [whole, (points, jnp.int32), (points, jnp.int32), (points, f32), (points, f32), ((ROWS, LANES), f32), ((16, LANES), jnp.int32)],
    )
    lists = [slot, where, other_core(column)]
    kept = [pltpu.VMEM((16, COLS), f32), pltpu.VMEM((FIELDS, ROWS, LANES), f32)]

    def ghost_tables(donors):
        (share,) = call(pick_kernel, [aux, donors] + lists, [((LANE_TILES + 2, 16, LANES), f32)])
        return [aux, share, other_core(share), cosine, sine, metric]

    row, side = ((FIELDS, 8, COLS), f32), ((FIELDS, ROWS, LANES), f32)
    totals = ((FIELDS,) + vreg, f32)
    states = [full]
    for factor in (time_step / 2, time_step / 2, time_step):
        if len(states) == 1:
            (inner,) = call(first_inner_kernel, [metric, full], [whole], cost=2_000_000)
            donors, inner = lax.optimization_barrier((donors, inner))
        else:
            pair = swap_packets(packet)
            now, inner = call(
                functools.partial(next_inner_kernel, factor), [aux, metric, full, inner] + rim, [whole, whole], cost=2_000_000
            )
            states[-1] = now
            pair, inner = lax.optimization_barrier((pair, inner))
            donors = spread_packets(pair)
        tables = ghost_tables(donors)
        (sums,) = call(donor_kernel, [aux, inner, index, weight], [totals], cost=500_000)
        *rim, packet = call(
            functools.partial(rim_kernel, factor),
            tables + [index, weight, sums, full, states[-1]],
            [row, side, packed],
            scratch=kept + [pltpu.VMEM(*totals)],
        )
        states.append(None)
    pair = swap_packets(packet)
    inner_shape = ((FIELDS, CT, COLS), f32)
    states[-1], base, inner = call(
        last_inner_kernel, [aux, metric] + states[:-1] + [inner] + rim, [whole, inner_shape, inner_shape], cost=2_000_000
    )
    pair, inner = lax.optimization_barrier((pair, inner))
    (result,) = call(
        last_rim_kernel,
        ghost_tables(spread_packets(pair)) + [base, inner, states[-1]],
        [((FIELDS, CT, CP), f32)],
        scratch=kept,
    )
    return result.reshape(state.shape)


def solution(mesh):
    fine = Mesh(mesh.devices.reshape(tuple(SIZES[a] for a in AXES)), AXES)
    return jax.shard_map(
        on_device,
        mesh=fine,
        in_specs=(
            P("panel", None, None, LAT, LON),
            P("panel", LAT, LON, None),
            P("panel", None, LAT, LON, None),
            P(None, None, LON),
            P(None, None, LAT),
            P(None, None, LON),
            P(None, None, LAT),
        ),
        out_specs=P("panel", None, None, LAT, LON),
        check_vma=False,
    )
```
